256 devices in a mesh: wide: 64 (over z, x, core), narrow: 4 (over y).
Axes of the slice: x: 4, y: 4, z: 8, core: 2. Of those that a mesh axis runs over, the one named last changes fastest.
Arguments:
- teacher_attn: bfloat16 [512, 2048], P(None, 'narrow'), may hold values from -60 to 60
- out_proj: bfloat16 [2048, 4608], P('narrow', 'wide'), may hold values from -0.125 to 0.125
- teacher_resid: bfloat16 [512, 4608], P(None, 'wide'), may hold values from -60 to 60
- norm_gains: float32 [2, 4608], replicated, may hold values from 0.5 to 1.5
- teacher_embed: bfloat16 [129024, 4608], P(('wide', 'narrow')), may hold values from -0.375 to 0.375
- student_hidden: bfloat16 [512, 3584], P('wide'), may hold values from -6 to 6
- student_embed: bfloat16 [129024, 3584], P(('wide', 'narrow')), may hold values from -0.375 to 0.375
- token_ids: int32 [512], replicated, may hold values from 0 to 129023
Outputs:
- loss: float32 [], replicated
- hidden_grad: float32 [512, 3584], P(('wide', 'narrow'))
- embed_grad: bfloat16 [129024, 3584], P(('wide', 'narrow'))
The draws below stay inside these ranges and needn't reach their ends.
All inputs are finite; a program needn't handle non-finite values.
Results may differ from the reference program's by a relative error of at most 0.0075.
Values may be sent and summed in bfloat16 or wider, within the bound.
A program may use at most 128 MiB of HBM per device.

```python
import math
import jax
import jax.numpy as jnp
import numpy as np
from jax import lax

TOKENS = 512
DT = 4608
HV = 2048
DS = 3584
VOCAB = 129024


def row_scales(key, count, lower, upper):
    return jnp.exp(jax.random.uniform(key, (count,), jnp.float32, jnp.log(lower), jnp.log(upper)))


def draw_teacher_attn(key, part):
    key = jax.random.fold_in(key, 11)
    key_rows, key_vals = jax.random.split(key)
    scales = row_scales(key_rows, TOKENS, 1.0, 10.0)
    values = jnp.clip(jax.random.normal(key_vals, (TOKENS, HV), jnp.float32), -6.0, 6.0)
    return (values * scales[:, None]).astype(jnp.bfloat16)


def draw_teacher_resid(key, part):
    key = jax.random.fold_in(key, 23)
    key_rows, key_vals = jax.random.split(key)
    scales = row_scales(key_rows, TOKENS, 0.3, 3.0)
    ramp = jnp.exp(jnp.log(3.0) * jnp.arange(DT, dtype=jnp.float32) / (DT - 1))
    values = jnp.clip(jax.random.normal(key_vals, (TOKENS, DT), jnp.float32), -6.0, 6.0)
    return (values * scales[:, None] * ramp[None, :]).astype(jnp.bfloat16)


def with_ends(array, key, low, largest):
    dims = array.shape
    spot = [jax.random.randint(jax.random.fold_in(key, axis), (), 0, dims[axis]) for axis in range(len(dims))]
    array = array.at[tuple(spot)].set(low)
    longest = dims.index(max(dims))
    spot[longest] = (spot[longest] + 1) % dims[longest]
    return array.at[tuple(spot)].set(largest)


def steps_of(own_key, dims, cuts, least, top_value):
    loudness = 1.0
    for position, parts in cuts:
        heights = jax.random.uniform(jax.random.fold_in(jax.random.fold_in(own_key, 6), position), (parts,), jnp.float32, least / len(cuts), top_value / len(cuts))
        loudness = loudness * jnp.repeat(jnp.exp(heights), dims[position] // parts).reshape((-1,) + (1,) * (len(dims) - 1 - position))
    return loudness


def skewed_wide(stream_key, dims, number_of, skew):
    portions = [min(1 << octave, number_of + 1 - (1 << octave)) * (1 << 20) // math.isqrt((1 << octave) ** skew) + 1 for octave in range((number_of + 1).bit_length()) if 1 << octave <= number_of]
    scale = 1 + sum(portions) // (1 << 30)
    grid = np.cumsum(np.array([max(1, weight // scale) for weight in portions]))
    ticket = jax.random.randint(jax.random.fold_in(stream_key, 1), dims, 0, int(grid[len(portions) - 1]))
    start = jnp.left_shift(1, jnp.searchsorted(jnp.asarray(grid, jnp.int32), ticket, side="right").astype(jnp.int32))
    standing = start - 1 + jax.random.randint(jax.random.fold_in(stream_key, 4), dims, 0, 1 << 30) % jnp.minimum(start, number_of + 1 - start)
    return jax.random.permutation(jax.random.fold_in(stream_key, 2), number_of)[standing].astype(jnp.int32)


def centred(rng, dims, width, most, cuts=(), kind=jnp.bfloat16):
    entries = jax.random.normal(rng, dims, jnp.float32) * width
    if len(cuts) > 0:
        entries = steps_of(rng, dims, cuts, -0.22, 0.18) * entries
    return jnp.clip(entries, min=-most, max=most).astype(kind)


def setup_inputs(seed: int = 0) -> dict:
    seeds = jax.random.split(jax.random.key(seed), 9)
    return {
        "teacher_attn": draw_teacher_attn(jax.random.fold_in(seeds[8], 71), 0),
        "out_proj": centred(seeds[1], (HV, DT), HV ** -0.5, 0.125, ((0, 4), (1, 64))),
        "teacher_resid": draw_teacher_resid(jax.random.fold_in(seeds[8], 71), 0),
        "norm_gains": jnp.clip(1.0 + 0.1 * jax.random.normal(seeds[3], (2, DT), jnp.float32), 0.5, 1.5),
        "teacher_embed": centred(seeds[4], (VOCAB, DT), (DT // 16) ** -0.5, 0.375, ((0, 256),)),
        "student_hidden": centred(seeds[5], (TOKENS, DS), 1.0, 6.0, ((0, 64),)),
        "student_embed": centred(seeds[6], (VOCAB, DS), (DS // 16) ** -0.5, 0.375, ((0, 256),)),
        "token_ids": with_ends(skewed_wide(seeds[7], (TOKENS,), VOCAB, 2), jax.random.fold_in(seeds[7], 3), 0, VOCAB - 1).astype(jnp.int32),
    }


def normalize(values):
    return values * lax.rsqrt(lax.optimization_barrier(jnp.mean(values * values, axis=-1, keepdims=True)) + 1e-06)

def capped(values):
    return 30.0 * jnp.tanh(values / 30.0)

def reference(teacher_attn, out_proj, teacher_resid, norm_gains, teacher_embed, student_hidden, student_embed, token_ids):
    attn_out = jnp.dot(teacher_attn, out_proj, preferred_element_type=jnp.float32).astype(jnp.bfloat16)
    attn_out = lax.optimization_barrier(attn_out).astype(jnp.float32)
    mixed = teacher_resid.astype(jnp.float32) + norm_gains[0] * normalize(attn_out)
    teacher_final = (norm_gains[1] * normalize(mixed)).astype(jnp.bfloat16)
    teach = capped(jnp.dot(teacher_final, teacher_embed.T, preferred_element_type=jnp.float32))
    stud = capped(jnp.dot(student_hidden, student_embed.T, preferred_element_type=jnp.float32))
    exp_teach = jnp.exp(teach - 30.0)
    exp_stud = jnp.exp(stud - 30.0)
    zt = lax.optimization_barrier(jnp.sum(exp_teach, axis=1))
    zs = lax.optimization_barrier(jnp.sum(exp_stud, axis=1))
    cross = lax.optimization_barrier(jnp.sum(exp_teach * (teach - stud), axis=1))
    columns = lax.broadcasted_iota(jnp.int32, stud.shape, 1)
    onehot = (columns == token_ids[:, None]).astype(jnp.float32)
    target = lax.optimization_barrier(jnp.sum(onehot * stud, axis=1))
    per_token = cross / zt - jnp.log(zt) + jnp.log(zs) + jnp.log(zs) + 30.0 - target
    loss = jnp.mean(per_token)
    grad_logit = 2.0 * exp_stud / zs[:, None] - exp_teach / zt[:, None] - onehot
    dz = (grad_logit * (1.0 - (stud / 30.0) ** 2) / TOKENS).astype(jnp.bfloat16)
    hidden_grad = jnp.dot(dz, student_embed, preferred_element_type=jnp.float32)
    embed_grad = jnp.dot(dz.T, student_hidden, preferred_element_type=jnp.float32).astype(jnp.bfloat16)
    return (loss, hidden_grad, embed_grad)
```

```python
import jax
import jax.numpy as jnp
from jax import lax
from jax.experimental import pallas as pl
from jax.experimental.pallas import tpu as pltpu
from jax.sharding import PartitionSpec as P

TOK, DT, DS, V, F = 512, 4608, 3584, 504, 72
NZ, NX, NY = 8, 4, 4
SA = 2048
TA = 80
HA = 2560
HB = DS - HA
NSEM = 192
MESH = pl.DeviceIdType.MESH
f32, bf16 = jnp.float32, jnp.bfloat16


def dot(a, b, ca, cb):
    return lax.dot_general(a, b, (((ca,), (cb,)), ((), ())), preferred_element_type=f32)


def kernel(
    attn_h, oproj_h, resid_h, gains_h, te_h, sh_h, se_h, ids_h,
    loss_o, hg_o, eg_o,
    attn, oproj, resid, gains, te, sh, se, ids,
    sf, tf, shx, shr, pt, pr, scale, sums, sums2, sr1, sr2, fx, fr,
    sb, tb, esb, etb, st, st2, st3, q1, q2, q3, dz,
    ho, hs, hr, hc, x1r, z1r, y1, y1b, z2r, x2r, fs0, fs1, fr0, fr1, eg,
    lsem, ss, rs,
):
    w = lax.axis_index("wide")
    y = lax.axis_index("narrow")
    z, x, c = w // 8, (w // 2) % 4, w % 2

    def dev(z_, x_, c_, y_):
        return ((z_ * 4 + x_) * 2 + c_, y_)

    def zp(k):
        return dev((z + k + NZ) % NZ, x, c, y)

    def xp(k):
        return dev(z, (x + k + NX) % NX, c, y)

    def yp(k):
        return dev(z, x, c, (y + k) % NY)

    def xcp(k):
        q = (x * 2 + c + k) % 8
        return dev(z, q // 2, q % 2, y)

    sib = dev(z, x, 1 - c, y)

    counter = [0]

    def sem():
        counter[0] += 1
        return counter[0] - 1

    class Copy:
        def __init__(self, src, dst, to, landing=None):
            self.src, self.dst, self.to, self.i = src, dst, to, sem()
            self.landing = dst if landing is None else landing

        def make(self, dst):
            return pltpu.make_async_remote_copy(
                src_ref=self.src, dst_ref=dst, send_sem=ss.at[self.i], recv_sem=rs.at[self.i],
                device_id=self.to, device_id_type=MESH,
            )

        def start(self):
            self.make(self.dst).start()

        def wait_send(self):
            self.make(self.dst).wait_send()

        def wait_recv(self):
            self.make(self.landing).wait_recv()

    def on_core(which, fn):
        pl.when(c == which)(fn)

    local = [
        pltpu.make_async_copy(a, b, lsem.at[i])
        for i, (a, b) in enumerate(
            [(sh_h, sh), (attn_h, attn), (oproj_h, oproj), (resid_h, resid), (gains_h, gains), (ids_h, ids), (se_h, se), (te_h, te)]
        )
    ]
    for cp in local:
        cp.start()

    barrier = pltpu.get_barrier_semaphore()
    peers = [zp(k) for k in range(1, 8)] + [xcp(k) for k in range(1, 8)] + [yp(k) for k in range(1, 4)]
    peers += [dev(z, x, 1 - c, (y + k) % NY) for k in range(1, 4)]
    for p in peers:
        pl.semaphore_signal(barrier, inc=1, device_id=p, device_id_type=MESH)
    local[0].wait()
    shx[...] = sh[...].astype(f32)
    pl.semaphore_wait(barrier, len(peers))

    c_sh = Copy(shx, shr, sib)
    c_sh.start()

    def ring(n, pos, peer, block, half):
        m = n // 2
        waits, starts, every = {}, {}, []
        for s in range(1, m + 1):
            last = s == m
            pick = half if last else (lambda i, h: block(i))
            r = Copy(pick((pos - s + 1 + n) % n, 0), pick((pos - s + 1 + n) % n, 0), peer(1), pick((pos - s + n) % n, 0))
            l = Copy(pick((pos + s - 1) % n, 1), pick((pos + s - 1) % n, 1), peer(-1), pick((pos + s) % n, 1))
            starts[s] = [r.start, l.start]
            waits[s] = [r.wait_recv, l.wait_recv]
            every += [r.wait_send, l.wait_send]
        return starts, waits, every

    def gather(buf, sel):
        def at(i, j, core, h=None):
            rows, cols = sel(core, h)
            return buf.at[i, j, rows, cols]

        every = slice(None)
        z0 = ring(NZ, z, zp, lambda i: at(i, x, 0), lambda i, h: at(i, x, 0, h))
        x0 = ring(NX, x, xp, lambda i: at(every, i, 0), lambda i, h: at(every, i, 0, h))
        x1 = ring(NX, x, xp, lambda i: at(z, i, 1), lambda i, h: at(z, i, 1, h))
        z1 = ring(NZ, z, zp, lambda i: at(i, every, 1), lambda i, h: at(i, every, 1, h))
        s0 = {k: Copy(at(every, (x + k + NX) % NX, 0), at(every, (x + k + NX) % NX, 0), sib) for k in (0, 1, -1, 2)}
        s1 = {
            k: Copy(at((z + k + NZ) % NZ, every, 1), at((z + k + NZ) % NZ, every, 1), sib)
            for k in (0, 1, -1, 2, -2, 3, -3, 4)
        }
        steps0 = [
            z0[0][1],
            z0[1][1] + z0[0][2],
            z0[1][2] + z0[0][3],
            z0[1][3] + z0[0][4],
            z0[1][4] + x0[0][1] + [s0[0].start],
            x0[1][1] + x0[0][2] + [s0[1].start, s0[-1].start],
            x0[1][2] + [s0[2].start],
            [s1[k].wait_recv for k in s1],
        ]
        steps1 = [
            x1[0][1],
            x1[1][1] + x1[0][2],
            x1[1][2] + z1[0][1] + [s1[0].start],
            z1[1][1] + z1[0][2] + [s1[1].start, s1[-1].start],
            z1[1][2] + z1[0][3] + [s1[2].start, s1[-2].start],
            z1[1][3] + z1[0][4] + [s1[3].start, s1[-3].start],
            z1[1][4] + [s1[4].start],
            [s0[k].wait_recv for k in s0],
        ]
        drain0 = z0[2] + x0[2] + [s0[k].wait_send for k in s0]
        drain1 = x1[2] + z1[2] + [s1[k].wait_send for k in s1]

        def emit(fns0, fns1):
            def run0():
                for fn in fns0:
                    fn()

            def run1():
                for fn in fns1:
                    fn()

            on_core(0, run0)
            on_core(1, run1)

        def gen():
            for a, b in zip(steps0, steps1):
                emit(a, b)
                yield

        return gen(), lambda: emit(drain0, drain1)

    def student_sel(core, h):
        lo, hi = (0, SA) if core == 0 else (SA, DS)
        if h is not None:
            mid = (lo + hi) // 2
            lo, hi = (lo, mid) if h == 0 else (mid, hi)
        return slice(None), pl.ds(lo, hi - lo)

    def teacher_sel(core, h):
        rows = pl.ds(0, TA) if core == 0 else pl.ds(TA, 2 * F - TA)
        return rows, slice(None) if h is None else pl.ds(h * 256, 256)

    student, student_drain = gather(sf, student_sel)
    teacher, teacher_drain = gather(tf, teacher_sel)

    local[1].wait()
    local[2].wait()
    proj = dot(oproj[...], attn[...], 0, 1)
    for b in range(NY):
        pt[b] = proj[:, b * 128 : (b + 1) * 128]
    c_pr = [Copy(pt.at[(y + k) % NY], pr.at[k - 1], yp(k)) for k in range(1, NY)]
    for cp in c_pr:
        cp.start()

    c_sh.wait_recv()
    first = jnp.where(c == 0, shx[...], shr[...])
    second = jnp.where(c == 0, shr[...], shx[...])
    block = jnp.concatenate([first, second], axis=0).astype(bf16)

    def put0():
        sf[z, x, :, 0:SA] = block[:, 0:SA]

    def put1():
        sf[z, x, :, SA:DS] = block[:, SA:DS]

    on_core(0, put0)
    on_core(1, put1)
    next(student)

    local[4].wait()
    feature = w * F + lax.broadcasted_iota(jnp.int32, (F, 512), 0)
    lane = lax.broadcasted_iota(jnp.int32, (F, 512), 1)

    def pick_gains(i, carry):
        part = gains[:, pl.ds(pl.multiple_of(i * 512, 512), 512)]
        here = (lane + i * 512) == feature
        g0 = carry[0] + jnp.sum(jnp.where(here, part[0:1, :], 0.0), axis=1, keepdims=True)
        g1 = carry[1] + jnp.sum(jnp.where(here, part[1:2, :], 0.0), axis=1, keepdims=True)
        return g0, g1

    zero_col = jnp.zeros((F, 1), f32)
    g0, g1 = lax.fori_loop(0, DT // 512, pick_gains, (zero_col, zero_col))
    local[3].wait()
    rows_here = resid[pl.ds(pl.multiple_of(y * 128, 128), 128), :]
    eye = (
        lax.broadcasted_iota(jnp.int32, (128, 128), 0) == lax.broadcasted_iota(jnp.int32, (128, 128), 1)
    ).astype(bf16)
    r = dot(rows_here, eye, 0, 0)

    for cp in c_pr:
        cp.wait_recv()
    a = pt[y] + pr[0] + pr[1] + pr[2]
    a = a.astype(bf16).astype(f32)
    ga = g0 * a
    sums[...] = jnp.zeros_like(sums)
    sums[0:1, :] = jnp.sum(a * a, axis=0, keepdims=True)
    sums[1:2, :] = jnp.sum(r * r, axis=0, keepdims=True)
    sums[2:3, :] = jnp.sum(r * ga, axis=0, keepdims=True)
    sums[3:4, :] = jnp.sum(ga * ga, axis=0, keepdims=True)
    c_s1 = [Copy(sums, sr1.at[k - 1], zp(k)) for k in range(1, 8)]
    for cp in c_s1:
        cp.start()
    next(student)
    for cp in c_s1:
        cp.wait_recv()
    sums2[...] = sums[...] + jnp.sum(sr1[...], axis=0)
    c_s2 = [Copy(sums2, sr2.at[k - 1], xcp(k)) for k in range(1, 8)]
    for cp in c_s2:
        cp.start()
    next(student)
    for cp in c_s2:
        cp.wait_recv()
    total = sums2[...] + jnp.sum(sr2[...], axis=0)
    post = lax.rsqrt(total[0:1, :] / DT + 1e-06)
    square = total[1:2, :] + 2.0 * post * total[2:3, :] + post * post * total[3:4, :]
    fin = lax.rsqrt(jnp.maximum(square, 0.0) / DT + 1e-06)
    final = g1 * ((r + ga * post) * fin)
    fx[...] = final
    c_f = Copy(fx, fr, sib)
    c_f.start()
    c_f.wait_recv()
    lo = jnp.where(c == 0, final, fr[...])
    hi = jnp.where(c == 0, fr[...], final)
    both = jnp.concatenate([lo, hi], axis=0).astype(bf16)
    mine = pl.ds(pl.multiple_of(y * 128, 128), 128)
    c_y0 = []
    c_y1 = []
    for k in range(1, NY):
        theirs = pl.ds(pl.multiple_of((y - k + NY) % NY * 128, 128), 128)
        for core, out in ((0, c_y0), (1, c_y1)):
            rows = teacher_sel(core, None)[0]
            out.append(Copy(tf.at[z, x, rows, mine], tf.at[z, x, rows, mine], yp(k), tf.at[z, x, rows, theirs]))

    def spread0():
        tf[z, x, 0:TA, mine] = both[0:TA]
        for cp in c_y0:
            cp.start()

    def spread1():
        tf[z, x, TA : 2 * F, mine] = both[TA : 2 * F]
        for cp in c_y1:
            cp.start()

    on_core(0, spread0)
    on_core(1, spread1)
    next(student)

    def spread_wait0():
        for cp in c_y0:
            cp.wait_recv()

    def spread_wait1():
        for cp in c_y1:
            cp.wait_recv()

    on_core(0, spread_wait0)
    on_core(1, spread_wait1)
    next(teacher)
    for _ in range(4):
        next(student)

    local[6].wait()
    for k in range(7):
        cols = slice(k * 512, (k + 1) * 512)
        part = dot(se[:, cols], sf[:, :, :, cols].reshape(TOK, 512), 1, 1)
        sb[...] = part if k == 0 else sb[...] + part
        next(teacher)

    local[7].wait()
    for k in range(4):
        part = dot(te[:, k * 1152 : (k + 1) * 1152], tf[2 * k : 2 * k + 2].reshape(1152, TOK), 1, 0)
        tb[...] = part if k == 0 else tb[...] + part

    local[5].wait()
    token = ids[...] - (w * NY + y) * V
    row = lax.broadcasted_iota(jnp.int32, (56, TOK), 0)

    def fold(v):
        return jnp.sum(v.reshape(7, 8, TOK), axis=0)

    def stats(i, carry):
        rows = pl.ds(pl.multiple_of(i * 56, 8), 56)
        s = 30.0 * jnp.tanh(sb[rows, :] / 30.0)
        t = 30.0 * jnp.tanh(tb[rows, :] / 30.0)
        es = jnp.exp(s - 30.0)
        et = jnp.exp(t - 30.0)
        sb[rows, :] = s
        esb[rows, :] = es
        etb[rows, :] = et
        hit = jnp.where(row + i * 56 == token, s, 0.0)
        return (
            carry[0] + fold(et),
            carry[1] + fold(es),
            carry[2] + fold(et * (t - s)),
            carry[3] + fold(hit),
        )

    zero = jnp.zeros((8, TOK), f32)
    accs = lax.fori_loop(0, V // 56, stats, (zero, zero, zero, zero))
    st[...] = jnp.zeros_like(st)
    for i in range(4):
        st[i : i + 1, :] = jnp.sum(accs[i], axis=0, keepdims=True)

    c_q1 = [Copy(st, q1.at[k - 1], zp(k)) for k in range(1, 8)]
    c_q2 = [Copy(st2, q2.at[k - 1], xcp(k)) for k in range(1, 8)]
    c_q3 = [Copy(st3, q3.at[k - 1], yp(k)) for k in range(1, 4)]
    for cp in c_q1:
        cp.start()
    for cp in c_q1:
        cp.wait_recv()
    st2[...] = st[...] + jnp.sum(q1[...], axis=0)
    for cp in c_q2:
        cp.start()
    for cp in c_q2:
        cp.wait_recv()
    st3[...] = st2[...] + jnp.sum(q2[...], axis=0)
    for cp in c_q3:
        cp.start()
    for cp in c_q3:
        cp.wait_recv()
    all_stats = st3[...] + jnp.sum(q3[...], axis=0)
    zt, zs = all_stats[0:1, :], all_stats[1:2, :]
    cross, target = all_stats[2:3, :], all_stats[3:4, :]
    log_zs = jnp.log(zs)
    per_token = cross / zt - jnp.log(zt) + log_zs + log_zs + 30.0 - target
    loss_o[...] = jnp.broadcast_to(jnp.sum(per_token, axis=1, keepdims=True) / TOK, loss_o.shape)

    scale[0:1, :] = 1.0 / zt
    scale[1:2, :] = 2.0 / zs
    for k in range(4):
        cols = slice(k * 128, (k + 1) * 128)
        s = sb[:, cols]
        row_all = lax.broadcasted_iota(jnp.int32, (V, 128), 0)
        onehot = (row_all == token[:, cols]).astype(f32)
        u = s / 30.0
        g = scale[1:2, cols] * esb[:, cols] - scale[0:1, cols] * etb[:, cols] - onehot
        dz[:, cols] = (g * (1.0 - u * u) / TOK).astype(bf16)

    def product(lo, n, out):
        def step(j, _):
            cols = pl.ds(pl.multiple_of(lo + j * 256, 256), 256)
            val = dot(dz[...], se[:, cols], 0, 0)
            out(pl.ds(pl.multiple_of(j * 256, 256), 256), val.reshape(NZ, NX, 16, 256))
            return 0

        lax.fori_loop(0, n // 256, step, 0)

    def out_send(cols, val):
        hs[:, :, :, cols] = val.astype(bf16)

    def out_own(cols, val):
        ho[:, :, :, cols] = val

    every = slice(None)
    chunks0 = [pl.ds(j * 512, 512) for j in range(HA // 512)]
    c_d0 = [Copy(hs.at[every, every, every, pl.ds(0, HB)], hr.at[every, every, every, pl.ds(0, HB)], sib)]
    c_d1 = [Copy(hs.at[every, every, every, ch], hr.at[every, every, every, ch], sib) for ch in chunks0]
    c_x1 = [
        [Copy(hc.at[every, (x + k) % NX, every, ch], x1r.at[k - 1, every, every, ch], xp(k)) for k in range(1, 4)]
        for ch in chunks0
    ]
    c_z1 = [Copy(hc.at[(z + k) % NZ, every, every, pl.ds(0, HB)], z1r.at[k - 1], zp(k)) for k in range(1, 8)]

    def grad0():
        product(HA, HB, out_send)
        c_d0[0].start()
        product(0, HA, out_own)
        for j, ch in enumerate(chunks0):
            cols = slice(j * 512, (j + 1) * 512)
            c_d1[j].wait_recv()
            val = ho[:, :, :, cols] + hr[:, :, :, cols].astype(f32)
            ho[:, :, :, cols] = val
            hc[:, :, :, cols] = val.astype(bf16)
            for cp in c_x1[j]:
                cp.start()

    def grad1():
        for j, ch in enumerate(chunks0):
            def one(cols, val, j=j):
                hs[:, :, :, pl.ds(pl.multiple_of(cols.start + j * 512, 256), 256)] = val.astype(bf16)

            product(j * 512, 512, one)
            c_d1[j].start()
        product(HA, HB, out_own)
        c_d0[0].wait_recv()
        val = ho[:, :, :, 0:HB] + hr[:, :, :, 0:HB].astype(f32)
        ho[:, :, :, 0:HB] = val
        hc[:, :, :, 0:HB] = val.astype(bf16)
        for cp in c_z1:
            cp.start()

    on_core(0, grad0)
    on_core(1, grad1)

    c_eg = []
    for k in range(7):
        cols = slice(k * 512, (k + 1) * 512)
        eg[:, cols] = dot(dz[...], sf[:, :, :, cols].reshape(TOK, 512), 1, 0).astype(bf16)
        c_eg.append(pltpu.make_async_copy(eg.at[:, pl.ds(k * 512, 512)], eg_o.at[:, pl.ds(k * 512, 512)], lsem.at[8 + k]))
        c_eg[k].start()

    c_z2 = [Copy(y1b.at[(z + k) % NZ], z2r.at[k - 1], zp(k)) for k in range(1, 8)]
    to = [(0, k) for k in range(4)] + [(1, k) for k in range(4)]

    def last(fs, frx, core):
        out = []
        for core_, k in to:
            if core_ == core and k == 0:
                continue
            yy = (y + k) % NY
            out.append(Copy(fs.at[pl.ds(8 * core_ + 2 * yy, 2)], frx.at[k], dev(z, x, core_, yy)))
        return out

    c_f0 = last(fs0, fr0, 0)
    c_f1 = last(fs1, fr1, 1)

    def second0():
        for j in range(len(chunks0)):
            for cp in c_x1[j]:
                cp.wait_recv()
        for j in range(len(chunks0)):
            cols = slice(j * 512, (j + 1) * 512)
            val = ho[:, x, :, cols]
            for k in range(3):
                val = val + x1r[k, :, :, cols].astype(f32)
            y1[:, :, cols] = val
            y1b[:, :, cols] = val.astype(bf16)
        for cp in c_z2:
            cp.start()
        for cp in c_z2:
            cp.wait_recv()
        val = y1[z]
        for k in range(7):
            val = val + z2r[k].astype(f32)
        for t in range(HA // 128):
            fs0[:, t, :] = val[:, t * 128 : (t + 1) * 128]
        for cp in c_f0:
            cp.start()
        fr0[0] = fs0[pl.ds(2 * y, 2)]

    c_x2b = [Copy(y1b.at[(x + k) % NX, every, pl.ds(0, HB)], x2r.at[k - 1], xp(k)) for k in range(1, 4)]

    def second1():
        for cp in c_z1:
            cp.wait_recv()
        val = ho[z, :, :, 0:HB]
        for k in range(7):
            val = val + z1r[k].astype(f32)
        y1[0:NX, :, 0:HB] = val
        y1b[0:NX, :, 0:HB] = val.astype(bf16)
        for cp in c_x2b:
            cp.start()
        for cp in c_x2b:
            cp.wait_recv()
        val = y1[x, :, 0:HB]
        for k in range(3):
            val = val + x2r[k].astype(f32)
        for t in range(HB // 128):
            fs1[:, t, :] = val[:, t * 128 : (t + 1) * 128]
        for cp in c_f1:
            cp.start()
        fr1[0] = fs1[pl.ds(8 + 2 * y, 2)]

    on_core(0, second0)
    on_core(1, second1)

    def arrive(frx, k, i):
        pltpu.make_async_remote_copy(
            src_ref=frx.at[k], dst_ref=frx.at[k], send_sem=ss.at[i], recv_sem=rs.at[i], device_id=sib, device_id_type=MESH
        ).wait_recv()

    def index_of(copies, core, core_, k):
        order = [(a, b) for a, b in to if not (a == core and b == 0)]
        return copies[order.index((core_, k))].i

    def arrive_on(core):
        def fn():
            for k in range(4):
                if not (core == 0 and k == 0):
                    arrive(fr0, k, index_of(c_f0, 0, core, k))
                if not (core == 1 and k == 0):
                    arrive(fr1, k, index_of(c_f1, 1, core, k))

        return fn

    on_core(0, arrive_on(0))
    on_core(1, arrive_on(1))
    hg_o[:, 0 : HA // 128, :] = jnp.sum(fr0[...], axis=0)
    hg_o[:, HA // 128 : DS // 128, :] = jnp.sum(fr1[...], axis=0)

    student_drain()
    teacher_drain()
    for cp in [c_sh, c_f] + c_pr + c_s1 + c_s2 + c_q1 + c_q2 + c_q3:
        cp.wait_send()

    def end0():
        for cp in c_y0 + c_d0 + [b for a_ in c_x1 for b in a_] + c_z2 + c_f0:
            cp.wait_send()

    def end1():
        for cp in c_y1 + c_d1 + c_z1 + c_x2b + c_f1:
            cp.wait_send()

    on_core(0, end0)
    on_core(1, end1)
    for cp in c_eg:
        cp.wait()
    assert counter[0] <= NSEM


def body(teacher_attn, out_proj, teacher_resid, norm_gains, teacher_embed, student_hidden, student_embed, token_ids):
    hbm = pl.BlockSpec(memory_space=pl.ANY)
    vm = pl.BlockSpec(memory_space=pltpu.VMEM)
    v = pltpu.VMEM
    loss, hg, eg = pl.pallas_call(
        kernel,
        out_shape=(
            jax.ShapeDtypeStruct((8, 128), f32),
            jax.ShapeDtypeStruct((2, DS // 128, 128), f32),
            jax.ShapeDtypeStruct((V, DS), bf16),
        ),
        in_specs=[hbm] * 8,
        out_specs=(vm, vm, hbm),
        scratch_shapes=[
            v((TOK, 512), bf16), v((512, F), bf16), v((TOK, F), bf16), v((2, DT), f32),
            v((V, DT), bf16), v((8, DS), bf16), v((V, DS), bf16), v((1, TOK), jnp.int32),
            v((NZ, NX, 16, DS), bf16), v((NZ, NX, 2 * F, TOK), bf16),
            v((8, DS), f32), v((8, DS), f32),
            v((NY, F, 128), f32), v((NY - 1, F, 128), f32), v((8, TOK), f32),
            v((8, 128), f32), v((8, 128), f32), v((7, 8, 128), f32), v((7, 8, 128), f32),
            v((F, 128), f32), v((F, 128), f32),
            v((V, TOK), f32), v((V, TOK), f32), v((V, TOK), f32), v((V, TOK), f32),
            v((8, TOK), f32), v((8, TOK), f32), v((8, TOK), f32),
            v((7, 8, TOK), f32), v((7, 8, TOK), f32), v((3, 8, TOK), f32),
            v((V, TOK), bf16),
            v((NZ, NX, 16, HA), f32), v((NZ, NX, 16, HA), bf16), v((NZ, NX, 16, HA), bf16), v((NZ, NX, 16, HA), bf16),
            v((3, NZ, 16, HA), bf16), v((7, NX, 16, HB), bf16),
            v((NZ, 16, HA), f32), v((NZ, 16, HA), bf16), v((7, 16, HA), bf16), v((4, 16, HB), bf16),
            v((16, HA // 128, 128), f32), v((16, HB // 128, 128), f32),
            v((4, 2, HA // 128, 128), f32), v((4, 2, HB // 128, 128), f32),
            v((V, DS), bf16),
            pltpu.SemaphoreType.DMA((15,)),
            pltpu.SemaphoreType.DMA((NSEM,)),
            pltpu.SemaphoreType.DMA((NSEM,)),
        ],
        compiler_params=pltpu.CompilerParams(
            collective_id=0, has_side_effects=True, vmem_limit_bytes=60 * 2**20
        ),
        name="step",
    )(
        teacher_attn, out_proj, teacher_resid, norm_gains, teacher_embed, student_hidden, student_embed,
        token_ids.reshape(1, TOK),
    )
    return loss[0, 0], hg.reshape(2, DS), eg


def solution(mesh):
    in_specs = (
        P(None, "narrow"),
        P("narrow", "wide"),
        P(None, "wide"),
        P(),
        P(("wide", "narrow"), None),
        P("wide", None),
        P(("wide", "narrow"), None),
        P(),
    )
    out_specs = (P(), P(("wide", "narrow"), None), P(("wide", "narrow"), None))
    return jax.shard_map(body, mesh=mesh, in_specs=in_specs, out_specs=out_specs, check_vma=False)
```

```python
import jax
import jax.numpy as jnp
from jax import lax
from jax.experimental import pallas as pl
from jax.experimental.pallas import tpu as pltpu
from jax.sharding import PartitionSpec as P

TOK, DT, DS, V, F = 512, 4608, 3584, 504, 72
NZ, NX, NY = 8, 4, 4
SA = 1792
TA = 64
HA = 2560
HB = DS - HA
NSEM = 320
MESH = pl.DeviceIdType.MESH
f32, bf16 = jnp.float32, jnp.bfloat16


def dot(a, b, ca, cb):
    return lax.dot_general(a, b, (((ca,), (cb,)), ((), ())), preferred_element_type=f32)


def kernel(
    attn_h, oproj_h, resid_h, gains_h, te_h, sh_h, se_h, ids_h,
    loss_o, hg_o, eg_o,
    attn, oproj, resid, gains, te, sh, se, ids,
    sf, tf, shx, shr, pt, pr, scale, sums, sums2, sums3, sr1, sr2, fx, fr,
    sb, tb, esb, etb, st, st2, st3, q1, q2, q3, dz, dzt,
    ho, hs, hr, hc, x1r, za, zb, ta, tb2, y1, y1b, z2r, x2r, fs0, fs1, fr0, fr1, eg,
    lsem, ss, rs,
):
    w = lax.axis_index("wide")
    y = lax.axis_index("narrow")
    z, x, c = w // 8, (w // 2) % 4, w % 2

    def dev(z_, x_, c_, y_):
        return ((z_ * 4 + x_) * 2 + c_, y_)

    def zp(k):
        return dev((z + k + NZ) % NZ, x, c, y)

    def xp(k):
        return dev(z, (x + k + NX) % NX, c, y)

    def yp(k):
        return dev(z, x, c, (y + k) % NY)

    def xyp(k):
        return dev(z, (x + k // 4) % NX, c, (y + k) % NY)

    sib = dev(z, x, 1 - c, y)

    counter = [0]

    def sem():
        counter[0] += 1
        return counter[0] - 1

    class Copy:
        def __init__(self, src, dst, to, landing=None):
            self.src, self.dst, self.to, self.i = src, dst, to, sem()
            self.landing = dst if landing is None else landing

        def make(self, dst):
            return pltpu.make_async_remote_copy(
                src_ref=self.src, dst_ref=dst, send_sem=ss.at[self.i], recv_sem=rs.at[self.i],
                device_id=self.to, device_id_type=MESH,
            )

        def start(self):
            self.make(self.dst).start()

        def wait_send(self):
            self.make(self.dst).wait_send()

        def wait_recv(self):
            self.make(self.landing).wait_recv()

    def on_core(which, fn):
        pl.when(c == which)(fn)

    local = [
        pltpu.make_async_copy(a, b, lsem.at[i])
        for i, (a, b) in enumerate(
            [(sh_h, sh), (attn_h, attn), (oproj_h, oproj), (resid_h, resid), (gains_h, gains), (ids_h, ids), (se_h, se), (te_h, te)]
        )
    ]
    for cp in local:
        cp.start()

    barrier = pltpu.get_barrier_semaphore()
    peers = [zp(k) for k in range(1, 8)] + [xyp(k) for k in range(1, 16)] + [sib]
    peers += [dev(z, x, 1 - c, (y + k) % NY) for k in range(1, 4)]
    for p in peers:
        pl.semaphore_signal(barrier, inc=1, device_id=p, device_id_type=MESH)
    local[0].wait()
    shx[...] = sh[...].astype(f32)
    pl.semaphore_wait(barrier, len(peers))

    c_sh = Copy(shx, shr, sib)
    c_sh.start()

    def ring(n, pos, peer, block, half):
        m = n // 2
        waits, starts, every = {}, {}, []
        for s in range(1, m + 1):
            last = s == m
            pick = half if last else (lambda i, h: block(i))
            r = Copy(pick((pos - s + 1 + n) % n, 0), pick((pos - s + 1 + n) % n, 0), peer(1), pick((pos - s + n) % n, 0))
            l = Copy(pick((pos + s - 1) % n, 1), pick((pos + s - 1) % n, 1), peer(-1), pick((pos + s) % n, 1))
            starts[s] = [r.start, l.start]
            waits[s] = [r.wait_recv, l.wait_recv]
            every += [r.wait_send, l.wait_send]
        return starts, waits, every

    near = (1, -1, 2, -2, 3, -3, 4)

    def gather(buf, sel):
        def at(i, j, core, h=None):
            rows, cols = sel(core, h)
            return buf.at[i, j, rows, cols]

        every = slice(None)

        def zi(k):
            return (z + k + NZ) % NZ

        def xi(k):
            return (x + k + NX) % NX

        z0 = ring(NZ, z, zp, lambda i: at(i, x, 0), lambda i, h: at(i, x, 0, h))
        x0 = {
            (d, k): Copy(at(zi(d), x, 0), at(zi(d), x, 0), xp(k), at(zi(d), xi(-k), 0))
            for d in (0,) + near for k in (1, 2, 3)
        }
        s0 = {k: Copy(at(every, xi(-k), 0), at(every, xi(-k), 0), sib) for k in (0, 1, 3, 2)}

        def fan(*ds):
            return [x0[d, k].start for d in ds for k in (1, 3, 2)]

        def landed(k):
            return [x0[d, k].wait_recv for d in (0,) + near]

        steps0 = [
            z0[0][1] + fan(0),
            z0[1][1] + z0[0][2] + fan(1, -1),
            z0[1][2] + z0[0][3] + fan(2, -2),
            z0[1][3] + z0[0][4] + fan(3, -3),
            z0[1][4] + fan(4) + [s0[0].start],
            landed(1) + [s0[1].start] + landed(3) + [s0[3].start],
            landed(2) + [s0[2].start],
        ]
        x1 = {k: Copy(at(z, x, 1), at(z, x, 1), xp(k), at(z, xi(-k), 1)) for k in (1, 3, 2)}
        z1 = {
            k: ring(NZ, z, zp, lambda i, k=k: at(i, xi(-k), 1), lambda i, h, k=k: at(i, xi(-k), 1, h)) for k in (0, 1, 3, 2)
        }
        s1 = {k: Copy(at(zi(k), every, 1), at(zi(k), every, 1), sib) for k in (0,) + near}

        def onward(n):
            out = []
            for k in (0, 1, 3, 2):
                out += z1[k][1][n]
                if n < 4:
                    out += z1[k][0][n + 1]
            return out

        steps1 = [
            [x1[k].start for k in x1] + z1[0][0][1],
            sum([[x1[k].wait_recv] + z1[k][0][1] for k in x1], []) + [s1[0].start],
            onward(1) + [s1[1].start, s1[-1].start],
            onward(2) + [s1[2].start, s1[-2].start],
            onward(3) + [s1[3].start, s1[-3].start],
            onward(4) + [s1[4].start],
            [],
        ]
        steps0.append([s1[k].wait_recv for k in s1])
        steps1.append([s0[k].wait_recv for k in s0])
        drain0 = z0[2] + [x0[i].wait_send for i in x0] + [s0[k].wait_send for k in s0]
        drain1 = [x1[k].wait_send for k in x1] + sum([z1[k][2] for k in z1], []) + [s1[k].wait_send for k in s1]

        def emit(fns0, fns1):
            def run0():
                for fn in fns0:
                    fn()

            def run1():
                for fn in fns1:
                    fn()

            on_core(0, run0)
            on_core(1, run1)

        def gen():
            for a, b in zip(steps0, steps1):
                emit(a, b)
                yield

        return gen(), lambda: emit(drain0, drain1)

    def student_sel(core, h):
        lo, hi = (0, SA) if core == 0 else (SA, DS)
        if h is not None:
            mid = (lo + hi) // 2
            lo, hi = (lo, mid) if h == 0 else (mid, hi)
        return slice(None), pl.ds(lo, hi - lo)

    def teacher_sel(core, h):
        rows = pl.ds(0, TA) if core == 0 else pl.ds(TA, 2 * F - TA)
        return rows, slice(None) if h is None else pl.ds(h * 256, 256)

    student, student_drain = gather(sf, student_sel)
    teacher, teacher_drain = gather(tf, teacher_sel)

    local[1].wait()
    local[2].wait()
    proj = dot(oproj[...], attn[...], 1, 1)
    for b in range(NY):
        pt[b] = proj[:, b * 128 : (b + 1) * 128]
    c_pr = [Copy(pt.at[(y + k) % NY], pr.at[k - 1], yp(k)) for k in range(1, NY)]
    for cp in c_pr:
        cp.start()

    c_sh.wait_recv()
    first = jnp.where(c == 0, shx[...], shr[...])
    second = jnp.where(c == 0, shr[...], shx[...])
    block = jnp.concatenate([first, second], axis=0).astype(bf16)

    def put0():
        sf[z, x, :, 0:SA] = block[:, 0:SA]

    def put1():
        sf[z, x, :, SA:DS] = block[:, SA:DS]

    on_core(0, put0)
    on_core(1, put1)
    next(student)

    local[4].wait()
    feature = w * F + lax.broadcasted_iota(jnp.int32, (F, 512), 0)
    lane = lax.broadcasted_iota(jnp.int32, (F, 512), 1)

    def pick_gains(i, carry):
        part = gains[:, pl.ds(pl.multiple_of(i * 512, 512), 512)]
        here = (lane + i * 512) == feature
        g0 = carry[0] + jnp.sum(jnp.where(here, part[0:1, :], 0.0), axis=1, keepdims=True)
        g1 = carry[1] + jnp.sum(jnp.where(here, part[1:2, :], 0.0), axis=1, keepdims=True)
        return g0, g1

    zero_col = jnp.zeros((F, 1), f32)
    g0, g1 = lax.fori_loop(0, DT // 512, pick_gains, (zero_col, zero_col))
    local[3].wait()
    r = resid[:, pl.ds(pl.multiple_of(y * 128, 128), 128)].astype(f32)

    for cp in c_pr:
        cp.wait_recv()
    a = pt[y] + pr[0] + pr[1] + pr[2]
    a = a.astype(bf16).astype(f32)
    ga = g0 * a
    sums[...] = jnp.zeros_like(sums)
    sums[0:1, :] = jnp.sum(a * a, axis=0, keepdims=True)
    sums[1:2, :] = jnp.sum(r * r, axis=0, keepdims=True)
    sums[2:3, :] = jnp.sum(r * ga, axis=0, keepdims=True)
    sums[3:4, :] = jnp.sum(ga * ga, axis=0, keepdims=True)
    c_s1 = Copy(sums, sr1.at[0], sib)
    c_s1.start()
    c_s1.wait_recv()
    sums2[...] = sums[...] + sr1[0]
    c_s2 = [Copy(sums2, sr1.at[k], xp(k)) for k in range(1, 4)]
    for cp in c_s2:
        cp.start()
    next(student)
    for cp in c_s2:
        cp.wait_recv()
    sums3[...] = sums2[...] + sr1[1] + sr1[2] + sr1[3]
    c_s3 = [Copy(sums3, sr2.at[k - 1], zp(k)) for k in range(1, 8)]
    for cp in c_s3:
        cp.start()
    next(student)
    for cp in c_s3:
        cp.wait_recv()
    total = sums3[...] + jnp.sum(sr2[...], axis=0)
    post = lax.rsqrt(total[0:1, :] / DT + 1e-06)
    square = total[1:2, :] + 2.0 * post * total[2:3, :] + post * post * total[3:4, :]
    fin = lax.rsqrt(jnp.maximum(square, 0.0) / DT + 1e-06)
    final = g1 * ((r + ga * post) * fin)
    fx[...] = final
    c_f = Copy(fx, fr, sib)
    c_f.start()
    c_f.wait_recv()
    lo = jnp.where(c == 0, final, fr[...])
    hi = jnp.where(c == 0, fr[...], final)
    both = jnp.concatenate([lo, hi], axis=0).astype(bf16)
    mine = pl.ds(pl.multiple_of(y * 128, 128), 128)
    c_y0 = []
    c_y1 = []
    for k in range(1, NY):
        theirs = pl.ds(pl.multiple_of((y - k + NY) % NY * 128, 128), 128)
        for core, out in ((0, c_y0), (1, c_y1)):
            rows = teacher_sel(core, None)[0]
            out.append(Copy(tf.at[z, x, rows, mine], tf.at[z, x, rows, mine], yp(k), tf.at[z, x, rows, theirs]))

    def spread0():
        tf[z, x, 0:TA, mine] = both[0:TA]
        for cp in c_y0:
            cp.start()

    def spread1():
        tf[z, x, TA : 2 * F, mine] = both[TA : 2 * F]
        for cp in c_y1:
            cp.start()

    on_core(0, spread0)
    on_core(1, spread1)
    next(student)

    def spread_wait0():
        for cp in c_y0:
            cp.wait_recv()

    def spread_wait1():
        for cp in c_y1:
            cp.wait_recv()

    on_core(0, spread_wait0)
    on_core(1, spread_wait1)
    next(teacher)
    next(student)
    next(teacher)
    next(student)
    next(teacher)
    next(student)
    next(student)

    local[6].wait()
    for k in range(7):
        cols = slice(k * 512, (k + 1) * 512)
        part = dot(se[:, cols], sf[:, :, :, cols].reshape(TOK, 512), 1, 1)
        sb[...] = part if k == 0 else sb[...] + part
        if k < 5:
            next(teacher)

    local[7].wait()
    for k in range(4):
        part = dot(te[:, k * 1152 : (k + 1) * 1152], tf[2 * k : 2 * k + 2].reshape(1152, TOK), 1, 0)
        tb[...] = part if k == 0 else tb[...] + part

    local[5].wait()
    token = ids[...] - (w * NY + y) * V
    row = lax.broadcasted_iota(jnp.int32, (56, TOK), 0)

    def fold(v):
        return jnp.sum(v.reshape(7, 8, TOK), axis=0)

    def stats(i, carry):
        rows = pl.ds(pl.multiple_of(i * 56, 8), 56)
        s = 30.0 * jnp.tanh(sb[rows, :] / 30.0)
        t = 30.0 * jnp.tanh(tb[rows, :] / 30.0)
        es = jnp.exp(s - 30.0)
        et = jnp.exp(t - 30.0)
        sb[rows, :] = s
        esb[rows, :] = es
        etb[rows, :] = et
        hit = jnp.where(row + i * 56 == token, s, 0.0)
        return (
            carry[0] + fold(et),
            carry[1] + fold(es),
            carry[2] + fold(et * (t - s)),
            carry[3] + fold(hit),
        )

    zero = jnp.zeros((8, TOK), f32)
    accs = lax.fori_loop(0, V // 56, stats, (zero, zero, zero, zero))
    for i in range(4):
        total_i = jnp.sum(accs[i], axis=0, keepdims=True)
        st[i : i + 1, :] = total_i[:, 0:256]
        st[4 + i : 5 + i, :] = total_i[:, 256:512]
    c_q1 = Copy(st, q1, sib)
    c_q1.start()
    c_q1.wait_recv()
    st2[...] = st[...] + q1[...]
    c_q2 = [Copy(st2, q2.at[k - 1], xyp(k)) for k in range(1, 16)]
    for cp in c_q2:
        cp.start()
    for cp in c_q2:
        cp.wait_recv()
    st3[...] = st2[...] + jnp.sum(q2[...], axis=0)
    c_q3 = [Copy(st3, q3.at[k - 1], zp(k)) for k in range(1, 8)]
    for cp in c_q3:
        cp.start()
    for cp in c_q3:
        cp.wait_recv()
    packed = st3[...] + jnp.sum(q3[...], axis=0)
    all_stats = jnp.concatenate([packed[0:4], packed[4:8]], axis=1)
    zt, zs = all_stats[0:1, :], all_stats[1:2, :]
    cross, target = all_stats[2:3, :], all_stats[3:4, :]
    log_zs = jnp.log(zs)
    per_token = cross / zt - jnp.log(zt) + log_zs + log_zs + 30.0 - target
    loss_o[0, 0] = jnp.sum(per_token) / TOK

    scale[0:1, :] = 1.0 / zt
    scale[1:2, :] = 2.0 / zs
    for k in range(4):
        cols = slice(k * 128, (k + 1) * 128)
        s = sb[:, cols]
        row_all = lax.broadcasted_iota(jnp.int32, (V, 128), 0)
        onehot = (row_all == token[:, cols]).astype(f32)
        u = s / 30.0
        g = scale[1:2, cols] * esb[:, cols] - scale[0:1, cols] * etb[:, cols] - onehot
        g = g * (1.0 - u * u) / TOK
        dz[:, cols] = g.astype(bf16)
        dzt[cols, :] = g.T.astype(bf16)

    def product(lo, n, out):
        def step(j, _):
            cols = pl.ds(pl.multiple_of(lo + j * 256, 256), 256)
            val = dot(dzt[...], se[:, cols], 1, 0)
            out(pl.ds(pl.multiple_of(j * 256, 256), 256), val.reshape(NZ, NX, 16, 256))
            return 0

        lax.fori_loop(0, n // 256, step, 0)

    def out_send(cols, val):
        hs[:, :, :, cols] = val.astype(bf16)

    def out_own(cols, val):
        ho[:, :, :, cols] = val

    every = slice(None)
    chunks0 = [pl.ds(j * 512, 512) for j in range(HA // 512)]
    c_d0 = [Copy(hs.at[every, every, every, pl.ds(0, HB)], hr.at[every, every, every, pl.ds(0, HB)], sib)]
    c_d1 = [Copy(hs.at[every, every, every, ch], hr.at[every, every, every, ch], sib) for ch in chunks0]
    c_x1 = [
        [Copy(hc.at[every, (x + k) % NX, every, ch], x1r.at[k - 1, every, every, ch], xp(k)) for k in range(1, 4)]
        for ch in chunks0
    ]
    own_b = pl.ds(0, HB)
    half_b = (pl.ds(0, HB // 2), pl.ds(HB // 2, HB // 2))

    def zi(k):
        return (z + k + NZ) % NZ

    c_za = [Copy(hc.at[zi(4), every, every, half_b[0]], za.at[0, every, every, half_b[0]], zp(1))]
    c_zb = [Copy(hc.at[zi(4), every, every, half_b[1]], zb.at[0, every, every, half_b[1]], zp(-1))]
    for k in range(1, 4):
        c_za.append(Copy(ta.at[k - 1], za.at[k], zp(1)))
        c_zb.append(Copy(tb2.at[k - 1], zb.at[k], zp(-1)))

    def grad0():
        product(HA, HB, out_send)
        c_d0[0].start()
        product(0, HA, out_own)
        for j, ch in enumerate(chunks0):
            cols = slice(j * 512, (j + 1) * 512)
            c_d1[j].wait_recv()
            val = ho[:, :, :, cols] + hr[:, :, :, cols].astype(f32)
            ho[:, :, :, cols] = val
            hc[:, :, :, cols] = val.astype(bf16)
            for cp in c_x1[j]:
                cp.start()

    def grad1():
        for j, ch in enumerate(chunks0):
            def one(cols, val, j=j):
                hs[:, :, :, pl.ds(pl.multiple_of(cols.start + j * 512, 256), 256)] = val.astype(bf16)

            product(j * 512, 512, one)
            c_d1[j].start()
        product(HA, HB, out_own)
        c_d0[0].wait_recv()
        val = ho[:, :, :, 0:HB] + hr[:, :, :, 0:HB].astype(f32)
        ho[:, :, :, 0:HB] = val
        hc[:, :, :, 0:HB] = val.astype(bf16)
        c_za[0].start()
        c_zb[0].start()

    on_core(0, grad0)
    on_core(1, grad1)

    c_eg = []

    def embed(k):
        cols = slice(k * 512, (k + 1) * 512)
        eg[:, cols] = dot(dz[...], sf[:, :, :, cols].reshape(TOK, 512), 1, 0).astype(bf16)
        c_eg.append(pltpu.make_async_copy(eg.at[:, pl.ds(k * 512, 512)], eg_o.at[:, pl.ds(k * 512, 512)], lsem.at[8 + k]))
        c_eg[k].start()

    c_z2 = [[Copy(y1b.at[(z + k) % NZ, every, ch], z2r.at[k - 1, every, ch], zp(k)) for k in range(1, 8)] for ch in chunks0]
    to = [(0, k) for k in range(4)] + [(1, k) for k in range(4)]

    def last(fs, frx, core):
        out = []
        for core_, k in to:
            if core_ == core and k == 0:
                continue
            yy = (y + k) % NY
            out.append(Copy(fs.at[pl.ds(8 * core_ + 2 * yy, 2)], frx.at[k], dev(z, x, core_, yy)))
        return out

    c_f0 = last(fs0, fr0, 0)
    c_f1 = last(fs1, fr1, 1)

    c_x2b = [Copy(y1b.at[(x + k) % NX, every, own_b], x2r.at[k - 1], xp(k)) for k in range(1, 4)]

    def first0(j):
        def fn():
            for cp in c_x1[j]:
                cp.wait_recv()
            cols = slice(j * 512, (j + 1) * 512)
            val = ho[:, x, :, cols]
            for k in range(3):
                val = val + x1r[k, :, :, cols].astype(f32)
            y1[:, :, cols] = val
            y1b[:, :, cols] = val.astype(bf16)
            for cp in c_z2[j]:
                cp.start()

        return fn

    def first1(n):
        def fn():
            c_za[n - 1].wait_recv()
            c_zb[n - 1].wait_recv()
            a_, b_ = half_b
            if n == 1:
                ta[0, :, :, a_] = (ho[zi(3), :, :, a_] + za[0, :, :, a_].astype(f32)).astype(bf16)
                ta[0, :, :, b_] = hc[zi(3), :, :, b_]
                tb2[0, :, :, a_] = hc[zi(-3), :, :, a_]
                tb2[0, :, :, b_] = (ho[zi(-3), :, :, b_] + zb[0, :, :, b_].astype(f32)).astype(bf16)
            else:
                ta[n - 1] = (ho[zi(4 - n), :, :, own_b] + za[n - 1].astype(f32)).astype(bf16)
                tb2[n - 1] = (ho[zi(n - 4), :, :, own_b] + zb[n - 1].astype(f32)).astype(bf16)
            c_za[n].start()
            c_zb[n].start()

        return fn

    def turn1():
        c_za[3].wait_recv()
        c_zb[3].wait_recv()
        val = ho[z, :, :, own_b] + za[3].astype(f32) + zb[3].astype(f32)
        y1[0:NX, :, own_b] = val
        y1b[0:NX, :, own_b] = val.astype(bf16)
        for cp in c_x2b:
            cp.start()

    def last1():
        for cp in c_x2b:
            cp.wait_recv()
        val = y1[x, :, 0:HB]
        for k in range(3):
            val = val + x2r[k].astype(f32)
        for t in range(HB // 128):
            fs1[:, t, :] = val[:, t * 128 : (t + 1) * 128]
        for cp in c_f1:
            cp.start()
        fr1[0] = fs1[pl.ds(8 + 2 * y, 2)]

    def last0():
        for j in range(len(chunks0)):
            for cp in c_z2[j]:
                cp.wait_recv()
            cols = slice(j * 512, (j + 1) * 512)
            val = y1[z, :, cols]
            for k in range(7):
                val = val + z2r[k, :, cols].astype(f32)
            for t in range(4):
                fs0[:, 4 * j + t, :] = val[:, t * 128 : (t + 1) * 128]
        for cp in c_f0:
            cp.start()
        fr0[0] = fs0[pl.ds(2 * y, 2)]

    for k in range(2):
        embed(k)
    for n, (f0, f1) in enumerate(
        [(first0(0), first1(1)), (first0(1), first1(2)), (first0(2), first1(3)), (first0(3), turn1), (first0(4), last1)]
    ):
        on_core(0, f0)
        on_core(1, f1)
        embed(2 + n)
    on_core(0, last0)

    def arrive(frx, k, i):
        pltpu.make_async_remote_copy(
            src_ref=frx.at[k], dst_ref=frx.at[k], send_sem=ss.at[i], recv_sem=rs.at[i], device_id=sib, device_id_type=MESH
        ).wait_recv()

    def index_of(copies, core, core_, k):
        order = [(a, b) for a, b in to if not (a == core and b == 0)]
        return copies[order.index((core_, k))].i

    def arrive_on(core):
        def fn():
            for k in range(4):
                if not (core == 0 and k == 0):
                    arrive(fr0, k, index_of(c_f0, 0, core, k))
                if not (core == 1 and k == 0):
                    arrive(fr1, k, index_of(c_f1, 1, core, k))

        return fn

    on_core(0, arrive_on(0))
    on_core(1, arrive_on(1))
    head = jnp.sum(fr0[...], axis=0)
    tail = jnp.sum(fr1[...], axis=0)
    for t in range(DS // 128):
        piece = head[:, t, :] if t < HA // 128 else tail[:, t - HA // 128, :]
        hg_o[:, t * 128 : (t + 1) * 128] = piece

    student_drain()
    teacher_drain()
    for cp in [c_sh, c_f, c_s1, c_q1] + c_pr + c_s2 + c_s3 + c_q2 + c_q3:
        cp.wait_send()

    def end0():
        for cp in c_y0 + c_d0 + [b for a_ in c_x1 + c_z2 for b in a_] + c_f0:
            cp.wait_send()

    def end1():
        for cp in c_y1 + c_d1 + c_za + c_zb + c_x2b + c_f1:
            cp.wait_send()

    on_core(0, end0)
    on_core(1, end1)
    for cp in c_eg:
        cp.wait()
    assert counter[0] <= NSEM


def body(teacher_attn, out_proj, teacher_resid, norm_gains, teacher_embed, student_hidden, student_embed, token_ids):
    hbm = pl.BlockSpec(memory_space=pl.ANY)
    vm = pl.BlockSpec(memory_space=pltpu.VMEM)
    v = pltpu.VMEM
    loss, hg, eg = pl.pallas_call(
        kernel,
        out_shape=(
            jax.ShapeDtypeStruct((1, 1), f32),
            jax.ShapeDtypeStruct((2, DS), f32),
            jax.ShapeDtypeStruct((V, DS), bf16),
        ),
        in_specs=[hbm] * 8,
        out_specs=(pl.BlockSpec(memory_space=pltpu.SMEM), vm, hbm),
        scratch_shapes=[
            v((TOK, 512), bf16), v((F, 512), bf16), v((F, TOK), bf16), v((2, DT), f32),
            v((V, DT), bf16), v((8, DS), bf16), v((V, DS), bf16), v((1, TOK), jnp.int32),
            v((NZ, NX, 16, DS), bf16), v((NZ, NX, 2 * F, TOK), bf16),
            v((8, DS), f32), v((8, DS), f32),
            v((NY, F, 128), f32), v((NY - 1, F, 128), f32), v((8, TOK), f32),
            v((8, 128), f32), v((8, 128), f32), v((8, 128), f32), v((4, 8, 128), f32), v((7, 8, 128), f32),
            v((F, 128), f32), v((F, 128), f32),
            v((V, TOK), f32), v((V, TOK), f32), v((V, TOK), f32), v((V, TOK), f32),
            v((8, 256), f32), v((8, 256), f32), v((8, 256), f32),
            v((8, 256), f32), v((15, 8, 256), f32), v((7, 8, 256), f32),
            v((V, TOK), bf16), v((TOK, V), bf16),
            v((NZ, NX, 16, HA), f32), v((NZ, NX, 16, HA), bf16), v((NZ, NX, 16, HA), bf16), v((NZ, NX, 16, HA), bf16),
            v((3, NZ, 16, HA), bf16),
            v((4, NX, 16, HB), bf16), v((4, NX, 16, HB), bf16), v((3, NX, 16, HB), bf16), v((3, NX, 16, HB), bf16),
            v((NZ, 16, HA), f32), v((NZ, 16, HA), bf16), v((7, 16, HA), bf16), v((4, 16, HB), bf16),
            v((16, HA // 128, 128), f32), v((16, HB // 128, 128), f32),
            v((4, 2, HA // 128, 128), f32), v((4, 2, HB // 128, 128), f32),
            v((V, DS), bf16),
            pltpu.SemaphoreType.DMA((15,)),
            pltpu.SemaphoreType.DMA((NSEM,)),
            pltpu.SemaphoreType.DMA((NSEM,)),
        ],
        compiler_params=pltpu.CompilerParams(
            collective_id=0, has_side_effects=True, vmem_limit_bytes=60 * 2**20
        ),
        name="step",
    )(
        teacher_attn, out_proj.T, teacher_resid.T, norm_gains, teacher_embed, student_hidden, student_embed,
        token_ids.reshape(1, TOK),
    )
    return loss.reshape(()), hg, eg


def solution(mesh):
    in_specs = (
        P(None, "narrow"),
        P("narrow", "wide"),
        P(None, "wide"),
        P(),
        P(("wide", "narrow"), None),
        P("wide", None),
        P(("wide", "narrow"), None),
        P(),
    )
    out_specs = (P(), P(("wide", "narrow"), None), P(("wide", "narrow"), None))
    return jax.shard_map(body, mesh=mesh, in_specs=in_specs, out_specs=out_specs, check_vma=False)
```

```python
import jax
import jax.numpy as jnp
from jax import lax
from jax.experimental import pallas as pl
from jax.experimental.pallas import tpu as pltpu
from jax.sharding import PartitionSpec as P

TOK, DT, DS, V, F = 512, 4608, 3584, 504, 72
NZ, NX, NY = 8, 4, 4
SA = 1792
TA = 64
HA = 2304
HB = DS - HA
NSEM = 320
MESH = pl.DeviceIdType.MESH
f32, bf16 = jnp.float32, jnp.bfloat16


def dot(a, b, ca, cb):
    return lax.dot_general(a, b, (((ca,), (cb,)), ((), ())), preferred_element_type=f32)


def kernel(
    attn_h, oproj_h, resid_h, gains_h, te_h, sh_h, se_h, ids_h,
    loss_o, hg_o, eg_o,
    attn, oproj, resid, gains, te, sh, se, ids,
    sf, tf, shx, shr, pt, pr, scale, sums2, sums3, sr1, sr2, rx, rr, ax, ar,
    sb, tb, esb, etb, st, st2, st3, q1, q2, q3, dz, dzt,
    ho, hs, hr, hc, x1r, za, zb, ta, tb2, y1, y1b, z2r, x2r, fs0, fs1, fr0, fr1, eg,
    lsem, ss, rs,
):
    w = lax.axis_index("wide")
    y = lax.axis_index("narrow")
    z, x, c = w // 8, (w // 2) % 4, w % 2

    def dev(z_, x_, c_, y_):
        return ((z_ * 4 + x_) * 2 + c_, y_)

    def zp(k):
        return dev((z + k + NZ) % NZ, x, c, y)

    def xp(k):
        return dev(z, (x + k + NX) % NX, c, y)

    def yp(k):
        return dev(z, x, c, (y + k) % NY)

    def xyp(k):
        return dev(z, (x + k // 4) % NX, c, (y + k) % NY)

    sib = dev(z, x, 1 - c, y)

    counter = [0]

    def sem():
        counter[0] += 1
        return counter[0] - 1

    class Copy:
        def __init__(self, src, dst, to, landing=None):
            self.src, self.dst, self.to, self.i = src, dst, to, sem()
            self.landing = dst if landing is None else landing

        def make(self, dst):
            return pltpu.make_async_remote_copy(
                src_ref=self.src, dst_ref=dst, send_sem=ss.at[self.i], recv_sem=rs.at[self.i],
                device_id=self.to, device_id_type=MESH,
            )

        def start(self):
            self.make(self.dst).start()

        def wait_send(self):
            self.make(self.dst).wait_send()

        def wait_recv(self):
            self.make(self.landing).wait_recv()

    def on_core(which, fn):
        pl.when(c == which)(fn)

    local = [
        pltpu.make_async_copy(a, b, lsem.at[i])
        for i, (a, b) in enumerate(
            [(sh_h, sh), (attn_h, attn), (oproj_h, oproj), (resid_h, resid), (gains_h, gains), (ids_h, ids), (se_h, se), (te_h, te)]
        )
    ]
    for cp in local:
        cp.start()

    barrier = pltpu.get_barrier_semaphore()
    peers = [zp(k) for k in range(1, 8)] + [xyp(k) for k in range(1, 16)] + [sib]
    peers += [dev(z, x, 1 - c, (y + k) % NY) for k in range(1, 4)]
    for p in peers:
        pl.semaphore_signal(barrier, inc=1, device_id=p, device_id_type=MESH)
    local[0].wait()
    shx[...] = sh[...].astype(f32)
    pl.semaphore_wait(barrier, len(peers))

    c_sh = Copy(shx, shr, sib)
    c_sh.start()
    local[3].wait()
    rx[...] = resid[:, pl.ds(pl.multiple_of(y * 128, 128), 128)].astype(f32)
    c_r = Copy(rx, rr, sib)
    c_r.start()

    def ring(n, pos, peer, block, half):
        m = n // 2
        waits, starts, every = {}, {}, []
        for s in range(1, m + 1):
            last = s == m
            pick = half if last else (lambda i, h: block(i))
            r = Copy(pick((pos - s + 1 + n) % n, 0), pick((pos - s + 1 + n) % n, 0), peer(1), pick((pos - s + n) % n, 0))
            l = Copy(pick((pos + s - 1) % n, 1), pick((pos + s - 1) % n, 1), peer(-1), pick((pos + s) % n, 1))
            starts[s] = [r.start, l.start]
            waits[s] = [r.wait_recv, l.wait_recv]
            every += [r.wait_send, l.wait_send]
        return starts, waits, every

    near = (1, -1, 2, -2, 3, -3, 4)

    def gather(buf, sel):
        def at(i, j, core, h=None):
            rows, cols = sel(core, h)
            return buf.at[i, j, rows, cols]

        every = slice(None)

        def zi(k):
            return (z + k + NZ) % NZ

        def xi(k):
            return (x + k + NX) % NX

        z0 = ring(NZ, z, zp, lambda i: at(i, x, 0), lambda i, h: at(i, x, 0, h))
        x0 = {
            (d, k): Copy(at(zi(d), x, 0), at(zi(d), x, 0), xp(k), at(zi(d), xi(-k), 0))
            for d in (0,) + near for k in (1, 2, 3)
        }
        s0 = {k: Copy(at(every, xi(-k), 0), at(every, xi(-k), 0), sib) for k in (0, 1, 3, 2)}

        def fan(*ds):
            return [x0[d, k].start for d in ds for k in (1, 3, 2)]

        def landed(k):
            return [x0[d, k].wait_recv for d in (0,) + near]

        steps0 = [
            z0[0][1] + fan(0),
            z0[1][1] + z0[0][2] + fan(1, -1),
            z0[1][2] + z0[0][3] + fan(2, -2),
            z0[1][3] + z0[0][4] + fan(3, -3),
            z0[1][4] + fan(4) + [s0[0].start],
            landed(1) + [s0[1].start] + landed(3) + [s0[3].start],
            landed(2) + [s0[2].start],
        ]
        x1 = {k: Copy(at(z, x, 1), at(z, x, 1), xp(k), at(z, xi(-k), 1)) for k in (1, 3, 2)}
        z1 = {
            k: ring(NZ, z, zp, lambda i, k=k: at(i, xi(-k), 1), lambda i, h, k=k: at(i, xi(-k), 1, h)) for k in (0, 1, 3, 2)
        }
        s1 = {k: Copy(at(zi(k), every, 1), at(zi(k), every, 1), sib) for k in (0,) + near}

        def onward(n):
            out = []
            for k in (0, 1, 3, 2):
                out += z1[k][1][n]
                if n < 4:
                    out += z1[k][0][n + 1]
            return out

        steps1 = [
            [x1[k].start for k in x1] + z1[0][0][1],
            sum([[x1[k].wait_recv] + z1[k][0][1] for k in x1], []) + [s1[0].start],
            onward(1) + [s1[1].start, s1[-1].start],
            onward(2) + [s1[2].start, s1[-2].start],
            onward(3) + [s1[3].start, s1[-3].start],
            onward(4) + [s1[4].start],
            [],
        ]
        steps0.append([s1[k].wait_recv for k in s1])
        steps1.append([s0[k].wait_recv for k in s0])
        drain0 = z0[2] + [x0[i].wait_send for i in x0] + [s0[k].wait_send for k in s0]
        drain1 = [x1[k].wait_send for k in x1] + sum([z1[k][2] for k in z1], []) + [s1[k].wait_send for k in s1]

        def emit(fns0, fns1):
            def run0():
                for fn in fns0:
                    fn()

            def run1():
                for fn in fns1:
                    fn()

            on_core(0, run0)
            on_core(1, run1)

        def gen():
            for a, b in zip(steps0, steps1):
                emit(a, b)
                yield

        return gen(), lambda: emit(drain0, drain1)

    def student_sel(core, h):
        lo, hi = (0, SA) if core == 0 else (SA, DS)
        if h is not None:
            mid = (lo + hi) // 2
            lo, hi = (lo, mid) if h == 0 else (mid, hi)
        return slice(None), pl.ds(lo, hi - lo)

    def teacher_sel(core, h):
        rows = pl.ds(0, TA) if core == 0 else pl.ds(TA, 2 * F - TA)
        return rows, slice(None) if h is None else pl.ds(h * 256, 256)

    student, student_drain = gather(sf, student_sel)
    teacher, teacher_drain = gather(tf, teacher_sel)

    local[1].wait()
    local[2].wait()
    proj = dot(oproj[...], attn[...], 1, 1)
    for b in range(NY):
        pt[b] = proj[:, b * 128 : (b + 1) * 128]
    c_pr = [Copy(pt.at[(y + k) % NY], pr.at[k - 1], yp(k)) for k in range(1, NY)]
    for cp in c_pr:
        cp.start()

    c_sh.wait_recv()
    first = jnp.where(c == 0, shx[...], shr[...])
    second = jnp.where(c == 0, shr[...], shx[...])
    block = jnp.concatenate([first, second], axis=0).astype(bf16)

    def put0():
        sf[z, x, :, 0:SA] = block[:, 0:SA]

    def put1():
        sf[z, x, :, SA:DS] = block[:, SA:DS]

    on_core(0, put0)
    on_core(1, put1)
    next(student)

    local[4].wait()
    feature = (w // 2) * 2 * F + lax.broadcasted_iota(jnp.int32, (2 * F, 128), 0)
    lane = lax.broadcasted_iota(jnp.int32, (2 * F, 128), 1)

    def pick_gains(i, carry):
        part = gains[:, pl.ds(pl.multiple_of(i * 128, 128), 128)]
        here = (lane + i * 128) == feature
        return carry[0] + jnp.where(here, part[0:1, :], 0.0), carry[1] + jnp.where(here, part[1:2, :], 0.0)

    none = jnp.zeros((2 * F, 128), f32)
    g0, g1 = lax.fori_loop(0, DT // 128, pick_gains, (none, none))
    g0 = jnp.sum(g0, axis=1, keepdims=True)
    g1 = jnp.sum(g1, axis=1, keepdims=True)
    next(student)

    def both_cores(own, other):
        return jnp.concatenate([jnp.where(c == 0, own, other), jnp.where(c == 0, other, own)], axis=0)

    for cp in c_pr:
        cp.wait_recv()
    a = pt[y] + pr[0] + pr[1] + pr[2]
    ax[...] = a.astype(bf16).astype(f32)
    c_a = Copy(ax, ar, sib)
    c_a.start()
    c_r.wait_recv()
    r = both_cores(rx[...], rr[...])
    c_a.wait_recv()
    a = both_cores(ax[...], ar[...])
    ga = g0 * a
    sums2[...] = jnp.zeros_like(sums2)
    sums2[0:1, :] = jnp.sum(a * a, axis=0, keepdims=True)
    sums2[1:2, :] = jnp.sum(r * r, axis=0, keepdims=True)
    sums2[2:3, :] = jnp.sum(r * ga, axis=0, keepdims=True)
    sums2[3:4, :] = jnp.sum(ga * ga, axis=0, keepdims=True)
    c_s2 = [Copy(sums2, sr1.at[k - 1], xp(k)) for k in range(1, 4)]
    for cp in c_s2:
        cp.start()
    next(student)
    for cp in c_s2:
        cp.wait_recv()
    sums3[...] = sums2[...] + sr1[0] + sr1[1] + sr1[2]
    c_s3 = [Copy(sums3, sr2.at[k - 1], zp(k)) for k in range(1, 8)]
    for cp in c_s3:
        cp.start()
    next(student)
    next(student)
    for cp in c_s3:
        cp.wait_recv()
    total = sums3[...] + jnp.sum(sr2[...], axis=0)
    post = lax.rsqrt(total[0:1, :] / DT + 1e-06)
    square = total[1:2, :] + 2.0 * post * total[2:3, :] + post * post * total[3:4, :]
    fin = lax.rsqrt(jnp.maximum(square, 0.0) / DT + 1e-06)
    final = g1 * ((r + ga * post) * fin)
    both = final.astype(bf16)
    mine = pl.ds(pl.multiple_of(y * 128, 128), 128)
    c_y0 = []
    c_y1 = []
    for k in range(1, NY):
        theirs = pl.ds(pl.multiple_of((y - k + NY) % NY * 128, 128), 128)
        for core, out in ((0, c_y0), (1, c_y1)):
            rows = teacher_sel(core, None)[0]
            out.append(Copy(tf.at[z, x, rows, mine], tf.at[z, x, rows, mine], yp(k), tf.at[z, x, rows, theirs]))

    def spread0():
        tf[z, x, 0:TA, mine] = both[0:TA]
        for cp in c_y0:
            cp.start()

    def spread1():
        tf[z, x, TA : 2 * F, mine] = both[TA : 2 * F]
        for cp in c_y1:
            cp.start()

    on_core(0, spread0)
    on_core(1, spread1)
    next(student)

    def spread_wait0():
        for cp in c_y0:
            cp.wait_recv()

    def spread_wait1():
        for cp in c_y1:
            cp.wait_recv()

    on_core(0, spread_wait0)
    on_core(1, spread_wait1)
    next(teacher)
    next(student)
    next(teacher)
    next(student)

    local[6].wait()
    for k in range(7):
        cols = slice(k * 512, (k + 1) * 512)
        part = dot(se[:, cols], sf[:, :, :, cols].reshape(TOK, 512), 1, 1)
        sb[...] = part if k == 0 else sb[...] + part
        if k < 6:
            next(teacher)

    local[7].wait()
    for k in range(4):
        part = dot(te[:, k * 1152 : (k + 1) * 1152], tf[2 * k : 2 * k + 2].reshape(1152, TOK), 1, 0)
        tb[...] = part if k == 0 else tb[...] + part

    local[5].wait()
    token = ids[...] - (w * NY + y) * V
    row = lax.broadcasted_iota(jnp.int32, (24, TOK), 0)

    def fold(v):
        return jnp.sum(v.reshape(3, 8, TOK), axis=0)

    def stats(i, carry):
        rows = pl.ds(pl.multiple_of(i * 24, 8), 24)
        u = jnp.tanh(sb[rows, :] * (1.0 / 30.0))
        s = 30.0 * u
        t = 30.0 * jnp.tanh(tb[rows, :] * (1.0 / 30.0))
        es = jnp.exp(s - 30.0)
        et = jnp.exp(t - 30.0)
        sb[rows, :] = 1.0 - u * u
        esb[rows, :] = es
        etb[rows, :] = et
        hit = jnp.where(row + i * 24 == token, s, 0.0)
        return (
            carry[0] + fold(et),
            carry[1] + fold(es),
            carry[2] + fold(et * (t - s)),
            carry[3] + fold(hit),
        )

    zero = jnp.zeros((8, TOK), f32)
    accs = lax.fori_loop(0, V // 24, stats, (zero, zero, zero, zero))
    for i in range(4):
        total_i = jnp.sum(accs[i], axis=0, keepdims=True)
        st[i : i + 1, :] = total_i[:, 0:256]
        st[4 + i : 5 + i, :] = total_i[:, 256:512]
    c_q1 = Copy(st, q1, sib)
    c_q1.start()
    c_q1.wait_recv()
    st2[...] = st[...] + q1[...]
    c_q2 = [Copy(st2, q2.at[k - 1], xyp(k)) for k in range(1, 16)]
    for cp in c_q2:
        cp.start()
    for cp in c_q2:
        cp.wait_recv()
    st3[...] = st2[...] + jnp.sum(q2[...], axis=0)
    c_q3 = [Copy(st3, q3.at[k - 1], zp(k)) for k in range(1, 8)]
    for cp in c_q3:
        cp.start()
    for cp in c_q3:
        cp.wait_recv()
    packed = st3[...] + jnp.sum(q3[...], axis=0)
    all_stats = jnp.concatenate([packed[0:4], packed[4:8]], axis=1)
    zt, zs = all_stats[0:1, :], all_stats[1:2, :]
    cross, target = all_stats[2:3, :], all_stats[3:4, :]
    log_zs = jnp.log(zs)
    per_token = cross / zt - jnp.log(zt) + log_zs + log_zs + 30.0 - target
    loss_o[0, 0] = jnp.sum(per_token) / TOK

    scale[0:1, :] = 1.0 / zt
    scale[1:2, :] = 2.0 / zs
    for k in range(4):
        cols = slice(k * 128, (k + 1) * 128)
        row_all = lax.broadcasted_iota(jnp.int32, (V, 128), 0)
        onehot = (row_all == token[:, cols]).astype(f32)
        g = scale[1:2, cols] * esb[:, cols] - scale[0:1, cols] * etb[:, cols] - onehot
        g = g * sb[:, cols] * (1.0 / TOK)
        dz[:, cols] = g.astype(bf16)
        dzt[cols, :] = g.T.astype(bf16)

    def product(lo, n, out):
        def step(j, _):
            cols = pl.ds(pl.multiple_of(lo + j * 256, 256), 256)
            val = dot(dzt[...], se[:, cols], 1, 0)
            out(pl.ds(pl.multiple_of(j * 256, 256), 256), val.reshape(NZ, NX, 16, 256))
            return 0

        lax.fori_loop(0, n // 256, step, 0)

    def out_send(cols, val):
        hs[:, :, :, cols] = val.astype(bf16)

    def out_own(cols, val):
        ho[:, :, :, cols] = val

    every = slice(None)
    chunks0 = [pl.ds(j, min(512, HA - j)) for j in range(0, HA, 512)]
    c_d0 = [Copy(hs.at[every, every, every, pl.ds(0, HB)], hr.at[every, every, every, pl.ds(0, HB)], sib)]
    c_d1 = [Copy(hs.at[every, every, every, ch], hr.at[every, every, every, ch], sib) for ch in chunks0]
    c_x1 = [
        [Copy(hc.at[every, (x + k) % NX, every, ch], x1r.at[k - 1, every, every, ch], xp(k)) for k in range(1, 4)]
        for ch in chunks0
    ]
    own_b = pl.ds(0, HB)
    half_b = (pl.ds(0, HB // 2), pl.ds(HB // 2, HB // 2))

    def zi(k):
        return (z + k + NZ) % NZ

    c_za = [Copy(hc.at[zi(4), every, every, half_b[0]], za.at[0, every, every, half_b[0]], zp(1))]
    c_zb = [Copy(hc.at[zi(4), every, every, half_b[1]], zb.at[0, every, every, half_b[1]], zp(-1))]
    for k in range(1, 4):
        c_za.append(Copy(ta.at[k - 1], za.at[k], zp(1)))
        c_zb.append(Copy(tb2.at[k - 1], zb.at[k], zp(-1)))

    def grad0():
        product(HA, HB, out_send)
        c_d0[0].start()
        for j, ch in enumerate(chunks0):
            lo, n = ch.start, ch.size

            def combine(i, _, lo=lo):
                cols = pl.ds(pl.multiple_of(lo + i * 256, 256), 256)
                val = dot(dzt[...], se[:, cols], 1, 0).reshape(NZ, NX, 16, 256)
                ho[:, :, :, cols] = val
                return 0

            lax.fori_loop(0, n // 256, combine, 0)
            c_d1[j].wait_recv()
            val = ho[:, :, :, ch] + hr[:, :, :, ch].astype(f32)
            ho[:, :, :, ch] = val
            hc[:, :, :, ch] = val.astype(bf16)
            for cp in c_x1[j]:
                cp.start()

    def grad1():
        def part(j):
            ch = chunks0[j]

            def one(cols, val):
                hs[:, :, :, pl.ds(pl.multiple_of(cols.start + ch.start, 256), 256)] = val.astype(bf16)

            product(ch.start, ch.size, one)
            c_d1[j].start()

        part(0)
        product(HA, HB, out_own)
        c_d0[0].wait_recv()
        val = ho[:, :, :, 0:HB] + hr[:, :, :, 0:HB].astype(f32)
        ho[:, :, :, 0:HB] = val
        hc[:, :, :, 0:HB] = val.astype(bf16)
        c_za[0].start()
        c_zb[0].start()
        for j in range(1, len(chunks0)):
            part(j)

    on_core(0, grad0)
    on_core(1, grad1)

    c_eg = []

    def embed(k):
        cols = slice(k * 512, (k + 1) * 512)
        eg[:, cols] = dot(dz[...], sf[:, :, :, cols].reshape(TOK, 512), 1, 0).astype(bf16)
        c_eg.append(pltpu.make_async_copy(eg.at[:, pl.ds(k * 512, 512)], eg_o.at[:, pl.ds(k * 512, 512)], lsem.at[8 + k]))
        c_eg[k].start()

    c_z2 = [[Copy(y1b.at[(z + k) % NZ, every, ch], z2r.at[k - 1, every, ch], zp(k)) for k in range(1, 8)] for ch in chunks0]
    to = [(0, k) for k in range(4)] + [(1, k) for k in range(4)]

    def last(fs, frx, core):
        out = []
        for core_, k in to:
            if core_ == core and k == 0:
                continue
            yy = (y + k) % NY
            out.append(Copy(fs.at[pl.ds(8 * core_ + 2 * yy, 2)], frx.at[k], dev(z, x, core_, yy)))
        return out

    c_f0 = last(fs0, fr0, 0)
    c_f1 = last(fs1, fr1, 1)

    c_x2b = [Copy(y1b.at[(x + k) % NX, every, own_b], x2r.at[k - 1], xp(k)) for k in range(1, 4)]

    def first0(j):
        def fn():
            for cp in c_x1[j]:
                cp.wait_recv()
            cols = chunks0[j]
            val = ho[:, x, :, cols]
            for k in range(3):
                val = val + x1r[k, :, :, cols].astype(f32)
            y1[:, :, cols] = val
            y1b[:, :, cols] = val.astype(bf16)
            for cp in c_z2[j]:
                cp.start()

        return fn

    def first1(n):
        def fn():
            c_za[n - 1].wait_recv()
            c_zb[n - 1].wait_recv()
            a_, b_ = half_b
            if n == 1:
                ta[0, :, :, a_] = (ho[zi(3), :, :, a_] + za[0, :, :, a_].astype(f32)).astype(bf16)
                ta[0, :, :, b_] = hc[zi(3), :, :, b_]
                tb2[0, :, :, a_] = hc[zi(-3), :, :, a_]
                tb2[0, :, :, b_] = (ho[zi(-3), :, :, b_] + zb[0, :, :, b_].astype(f32)).astype(bf16)
            else:
                ta[n - 1] = (ho[zi(4 - n), :, :, own_b] + za[n - 1].astype(f32)).astype(bf16)
                tb2[n - 1] = (ho[zi(n - 4), :, :, own_b] + zb[n - 1].astype(f32)).astype(bf16)
            c_za[n].start()
            c_zb[n].start()

        return fn

    def turn1():
        c_za[3].wait_recv()
        c_zb[3].wait_recv()
        val = ho[z, :, :, own_b] + za[3].astype(f32) + zb[3].astype(f32)
        y1[0:NX, :, own_b] = val
        y1b[0:NX, :, own_b] = val.astype(bf16)
        for cp in c_x2b:
            cp.start()

    def last1():
        for cp in c_x2b:
            cp.wait_recv()
        val = y1[x, :, 0:HB]
        for k in range(3):
            val = val + x2r[k].astype(f32)
        for t in range(HB // 128):
            fs1[:, t, :] = val[:, t * 128 : (t + 1) * 128]
        for cp in c_f1:
            cp.start()
        fr1[0] = fs1[pl.ds(8 + 2 * y, 2)]

    def last0():
        for j in range(len(chunks0)):
            for cp in c_z2[j]:
                cp.wait_recv()
            cols = chunks0[j]
            val = y1[z, :, cols]
            for k in range(7):
                val = val + z2r[k, :, cols].astype(f32)
            for t in range(cols.size // 128):
                fs0[:, 4 * j + t, :] = val[:, t * 128 : (t + 1) * 128]
        for cp in c_f0:
            cp.start()
        fr0[0] = fs0[pl.ds(2 * y, 2)]

    for k in range(2):
        embed(k)
    for n, (f0, f1) in enumerate(
        [(first0(0), first1(1)), (first0(1), first1(2)), (first0(2), first1(3)), (first0(3), turn1), (first0(4), last1)]
    ):
        on_core(0, f0)
        on_core(1, f1)
        embed(2 + n)
    on_core(0, last0)

    def arrive(frx, k, i):
        pltpu.make_async_remote_copy(
            src_ref=frx.at[k], dst_ref=frx.at[k], send_sem=ss.at[i], recv_sem=rs.at[i], device_id=sib, device_id_type=MESH
        ).wait_recv()

    def index_of(copies, core, core_, k):
        order = [(a, b) for a, b in to if not (a == core and b == 0)]
        return copies[order.index((core_, k))].i

    def arrive_on(core):
        def fn():
            for k in range(4):
                if not (core == 0 and k == 0):
                    arrive(fr0, k, index_of(c_f0, 0, core, k))
                if not (core == 1 and k == 0):
                    arrive(fr1, k, index_of(c_f1, 1, core, k))

        return fn

    on_core(0, arrive_on(0))
    on_core(1, arrive_on(1))
    head = jnp.sum(fr0[...], axis=0)
    tail = jnp.sum(fr1[...], axis=0)
    for t in range(DS // 128):
        piece = head[:, t, :] if t < HA // 128 else tail[:, t - HA // 128, :]
        hg_o[:, t * 128 : (t + 1) * 128] = piece

    student_drain()
    teacher_drain()
    for cp in [c_sh, c_r, c_a, c_q1] + c_pr + c_s2 + c_s3 + c_q2 + c_q3:
        cp.wait_send()

    def end0():
        for cp in c_y0 + c_d0 + [b for a_ in c_x1 + c_z2 for b in a_] + c_f0:
            cp.wait_send()

    def end1():
        for cp in c_y1 + c_d1 + c_za + c_zb + c_x2b + c_f1:
            cp.wait_send()

    on_core(0, end0)
    on_core(1, end1)
    for cp in c_eg:
        cp.wait()
    assert counter[0] <= NSEM


def body(teacher_attn, out_proj, teacher_resid, norm_gains, teacher_embed, student_hidden, student_embed, token_ids):
    hbm = pl.BlockSpec(memory_space=pl.ANY)
    vm = pl.BlockSpec(memory_space=pltpu.VMEM)
    v = pltpu.VMEM
    loss, hg, eg = pl.pallas_call(
        kernel,
        out_shape=(
            jax.ShapeDtypeStruct((1, 1), f32),
            jax.ShapeDtypeStruct((2, DS), f32),
            jax.ShapeDtypeStruct((V, DS), bf16),
        ),
        in_specs=[hbm] * 8,
        out_specs=(pl.BlockSpec(memory_space=pltpu.SMEM), vm, hbm),
        scratch_shapes=[
            v((TOK, 512), bf16), v((F, 512), bf16), v((F, TOK), bf16), v((2, DT), f32),
            v((V, DT), bf16), v((8, DS), bf16), v((V, DS), bf16), v((1, TOK), jnp.int32),
            v((NZ, NX, 16, DS), bf16), v((NZ, NX, 2 * F, TOK), bf16),
            v((8, DS), f32), v((8, DS), f32),
            v((NY, F, 128), f32), v((NY - 1, F, 128), f32), v((8, TOK), f32),
            v((8, 128), f32), v((8, 128), f32), v((3, 8, 128), f32), v((7, 8, 128), f32),
            v((F, 128), f32), v((F, 128), f32), v((F, 128), f32), v((F, 128), f32),
            v((V, TOK), f32), v((V, TOK), f32), v((V, TOK), f32), v((V, TOK), f32),
            v((8, 256), f32), v((8, 256), f32), v((8, 256), f32),
            v((8, 256), f32), v((15, 8, 256), f32), v((7, 8, 256), f32),
            v((V, TOK), bf16), v((TOK, V), bf16),
            v((NZ, NX, 16, HA), f32), v((NZ, NX, 16, HA), bf16), v((NZ, NX, 16, HA), bf16), v((NZ, NX, 16, HA), bf16),
            v((3, NZ, 16, HA), bf16),
            v((4, NX, 16, HB), bf16), v((4, NX, 16, HB), bf16), v((3, NX, 16, HB), bf16), v((3, NX, 16, HB), bf16),
            v((NZ, 16, HA), f32), v((NZ, 16, HA), bf16), v((7, 16, HA), bf16), v((4, 16, HB), bf16),
            v((16, HA // 128, 128), f32), v((16, HB // 128, 128), f32),
            v((4, 2, HA // 128, 128), f32), v((4, 2, HB // 128, 128), f32),
            v((V, DS), bf16),
            pltpu.SemaphoreType.DMA((15,)),
            pltpu.SemaphoreType.DMA((NSEM,)),
            pltpu.SemaphoreType.DMA((NSEM,)),
        ],
        compiler_params=pltpu.CompilerParams(
            collective_id=0, has_side_effects=True, vmem_limit_bytes=60 * 2**20
        ),
        name="step",
    )(
        teacher_attn, out_proj.T, teacher_resid.T, norm_gains, teacher_embed, student_hidden, student_embed,
        token_ids.reshape(1, TOK),
    )
    return loss.reshape(()), hg, eg


def solution(mesh):
    in_specs = (
        P(None, "narrow"),
        P("narrow", "wide"),
        P(None, "wide"),
        P(),
        P(("wide", "narrow"), None),
        P("wide", None),
        P(("wide", "narrow"), None),
        P(),
    )
    out_specs = (P(), P(("wide", "narrow"), None), P(("wide", "narrow"), None))
    return jax.shard_map(body, mesh=mesh, in_specs=in_specs, out_specs=out_specs, check_vma=False)
```

```python
import jax
import jax.numpy as jnp
from jax import lax
from jax.experimental import pallas as pl
from jax.experimental.pallas import tpu as pltpu
from jax.sharding import PartitionSpec as P

TOK, DT, DS, V, F = 512, 4608, 3584, 504, 72
NZ, NX, NY = 8, 4, 4
SA = 2048
TA = 80
HA = 2560
HB = DS - HA
NSEM = 320
MESH = pl.DeviceIdType.MESH
f32, bf16 = jnp.float32, jnp.bfloat16


def dot(a, b, ca, cb):
    return lax.dot_general(a, b, (((ca,), (cb,)), ((), ())), preferred_element_type=f32)


def kernel(
    attn_h, oproj_h, resid_h, gains_h, te_h, sh_h, se_h, ids_h,
    loss_o, hg_o, eg_o,
    attn, oproj, resid, gains, te, sh, se, ids,
    sf, tf, shx, shr, pt, pr, scale, sums2, sums3, sr1, sr2, rx, rr, ax, ar,
    sb, tb, esb, etb, st, st2, st3, q1, q2, q3, dz, dzt,
    hs, hr, hc, x1r, z1r, y1, y1b, z2r, x2r, fs0, fs1, fr0, fr1, eg,
    lsem, ss, rs,
):
    w = lax.axis_index("wide")
    y = lax.axis_index("narrow")
    z, x, c = w // 8, (w // 2) % 4, w % 2

    def dev(z_, x_, c_, y_):
        return ((z_ * 4 + x_) * 2 + c_, y_)

    def zp(k):
        return dev((z + k + NZ) % NZ, x, c, y)

    def xp(k):
        return dev(z, (x + k + NX) % NX, c, y)

    def yp(k):
        return dev(z, x, c, (y + k) % NY)

    def xyp(k):
        return dev(z, (x + k // 4) % NX, c, (y + k) % NY)

    sib = dev(z, x, 1 - c, y)

    counter = [0]

    def sem():
        counter[0] += 1
        return counter[0] - 1

    class Copy:
        def __init__(self, src, dst, to, landing=None):
            self.src, self.dst, self.to, self.i = src, dst, to, sem()
            self.landing = dst if landing is None else landing

        def make(self, dst):
            return pltpu.make_async_remote_copy(
                src_ref=self.src, dst_ref=dst, send_sem=ss.at[self.i], recv_sem=rs.at[self.i],
                device_id=self.to, device_id_type=MESH,
            )

        def start(self):
            self.make(self.dst).start()

        def wait_send(self):
            self.make(self.dst).wait_send()

        def wait_recv(self):
            self.make(self.landing).wait_recv()

    def on_core(which, fn):
        pl.when(c == which)(fn)

    local = [
        pltpu.make_async_copy(a, b, lsem.at[i])
        for i, (a, b) in enumerate(
            [(sh_h, sh), (attn_h, attn), (oproj_h, oproj), (resid_h, resid), (gains_h, gains), (ids_h, ids), (se_h, se), (te_h, te)]
        )
    ]
    for cp in local:
        cp.start()

    barrier = pltpu.get_barrier_semaphore()
    peers = [zp(k) for k in range(1, 8)] + [xyp(k) for k in range(1, 16)] + [sib]
    peers += [dev(z, x, 1 - c, (y + k) % NY) for k in range(1, 4)]
    for p in peers:
        pl.semaphore_signal(barrier, inc=1, device_id=p, device_id_type=MESH)
    local[0].wait()
    shx[...] = sh[...].astype(f32)
    c_sh = Copy(shx, shr, sib)
    local[3].wait()
    rx[...] = resid[:, pl.ds(pl.multiple_of(y * 128, 128), 128)].astype(f32)
    c_r = Copy(rx, rr, sib)

    def ring(n, pos, peer, block, half):
        m = n // 2
        waits, starts, every = {}, {}, []
        for s in range(1, m + 1):
            last = s == m
            pick = half if last else (lambda i, h: block(i))
            r = Copy(pick((pos - s + 1 + n) % n, 0), pick((pos - s + 1 + n) % n, 0), peer(1), pick((pos - s + n) % n, 0))
            l = Copy(pick((pos + s - 1) % n, 1), pick((pos + s - 1) % n, 1), peer(-1), pick((pos + s) % n, 1))
            starts[s] = [r.start, l.start]
            waits[s] = [r.wait_recv, l.wait_recv]
            every += [r.wait_send, l.wait_send]
        return starts, waits, every

    near = (1, -1, 2, -2, 3, -3, 4)

    def gather(buf, sel):
        def at(i, j, core, h=None):
            rows, cols = sel(core, h)
            return buf.at[i, j, rows, cols]

        every = slice(None)

        def zi(k):
            return (z + k + NZ) % NZ

        def xi(k):
            return (x + k + NX) % NX

        z0 = ring(NZ, z, zp, lambda i: at(i, x, 0), lambda i, h: at(i, x, 0, h))
        x0 = {
            (d, k): Copy(at(zi(d), x, 0), at(zi(d), x, 0), xp(k), at(zi(d), xi(-k), 0))
            for d in (0,) + near for k in (1, 2, 3)
        }
        s0 = {k: Copy(at(every, xi(-k), 0), at(every, xi(-k), 0), sib) for k in (0, 1, 3, 2)}

        def fan(*ds):
            return [x0[d, k].start for d in ds for k in (1, 3, 2)]

        def landed(k):
            return [x0[d, k].wait_recv for d in (0,) + near]

        steps0 = [
            z0[0][1] + fan(0),
            z0[1][1] + z0[0][2] + fan(1, -1),
            z0[1][2] + z0[0][3] + fan(2, -2),
            z0[1][3] + z0[0][4] + fan(3, -3),
            z0[1][4] + fan(4) + [s0[0].start],
            landed(1) + [s0[1].start] + landed(3) + [s0[3].start],
            landed(2) + [s0[2].start],
        ]
        x1 = {k: Copy(at(z, x, 1), at(z, x, 1), xp(k), at(z, xi(-k), 1)) for k in (1, 3, 2)}
        z1 = {
            k: ring(NZ, z, zp, lambda i, k=k: at(i, xi(-k), 1), lambda i, h, k=k: at(i, xi(-k), 1, h)) for k in (0, 1, 3, 2)
        }
        s1 = {k: Copy(at(zi(k), every, 1), at(zi(k), every, 1), sib) for k in (0,) + near}

        def onward(n):
            out = []
            for k in (0, 1, 3, 2):
                out += z1[k][1][n]
                if n < 4:
                    out += z1[k][0][n + 1]
            return out

        steps1 = [
            [x1[k].start for k in x1] + z1[0][0][1],
            sum([[x1[k].wait_recv] + z1[k][0][1] for k in x1], []) + [s1[0].start],
            onward(1) + [s1[1].start, s1[-1].start],
            onward(2) + [s1[2].start, s1[-2].start],
            onward(3) + [s1[3].start, s1[-3].start],
            onward(4) + [s1[4].start],
            [],
        ]
        steps0.append([s1[k].wait_recv for k in s1])
        steps1.append([s0[k].wait_recv for k in s0])
        drain0 = z0[2] + [x0[i].wait_send for i in x0] + [s0[k].wait_send for k in s0]
        drain1 = [x1[k].wait_send for k in x1] + sum([z1[k][2] for k in z1], []) + [s1[k].wait_send for k in s1]

        def emit(fns0, fns1):
            def run0():
                for fn in fns0:
                    fn()

            def run1():
                for fn in fns1:
                    fn()

            on_core(0, run0)
            on_core(1, run1)

        def gen():
            for a, b in zip(steps0, steps1):
                emit(a, b)
                yield

        return gen(), lambda: emit(drain0, drain1)

    def student_sel(core, h):
        lo, hi = (0, SA) if core == 0 else (SA, DS)
        if h is not None:
            mid = (lo + hi) // 2
            lo, hi = (lo, mid) if h == 0 else (mid, hi)
        return slice(None), pl.ds(lo, hi - lo)

    def teacher_sel(core, h):
        rows = pl.ds(0, TA) if core == 0 else pl.ds(TA, 2 * F - TA)
        return rows, slice(None) if h is None else pl.ds(h * 256, 256)

    student, student_drain = gather(sf, student_sel)
    teacher, teacher_drain = gather(tf, teacher_sel)

    local[1].wait()
    local[2].wait()
    proj = dot(oproj[...], attn[...], 1, 1)
    for b in range(NY):
        pt[b] = proj[:, b * 128 : (b + 1) * 128]
    c_pr = [Copy(pt.at[(y + k) % NY], pr.at[k - 1], yp(k)) for k in range(1, NY)]
    local[4].wait()
    feature = (w // 2) * 2 * F + lax.broadcasted_iota(jnp.int32, (2 * F, 128), 0)
    lane = lax.broadcasted_iota(jnp.int32, (2 * F, 128), 1)

    def pick_gains(i, carry):
        part = gains[:, pl.ds(pl.multiple_of(i * 128, 128), 128)]
        here = (lane + i * 128) == feature
        return carry[0] + jnp.where(here, part[0:1, :], 0.0), carry[1] + jnp.where(here, part[1:2, :], 0.0)

    none = jnp.zeros((2 * F, 128), f32)
    g0, g1 = lax.fori_loop(0, DT // 128, pick_gains, (none, none))
    g0 = jnp.sum(g0, axis=1, keepdims=True)
    g1 = jnp.sum(g1, axis=1, keepdims=True)

    pl.semaphore_wait(barrier, len(peers))
    c_sh.start()
    for cp in c_pr:
        cp.start()
    c_r.start()

    c_sh.wait_recv()
    first = jnp.where(c == 0, shx[...], shr[...])
    second = jnp.where(c == 0, shr[...], shx[...])
    block = jnp.concatenate([first, second], axis=0).astype(bf16)

    def put0():
        sf[z, x, :, 0:SA] = block[:, 0:SA]

    def put1():
        sf[z, x, :, SA:DS] = block[:, SA:DS]

    on_core(0, put0)
    on_core(1, put1)
    next(student)

    def both_cores(own, other):
        return jnp.concatenate([jnp.where(c == 0, own, other), jnp.where(c == 0, other, own)], axis=0)

    for cp in c_pr:
        cp.wait_recv()
    a = pt[y] + pr[0] + pr[1] + pr[2]
    ax[...] = a.astype(bf16).astype(f32)
    c_a = Copy(ax, ar, sib)
    c_a.start()
    c_r.wait_recv()
    r = both_cores(rx[...], rr[...])
    c_a.wait_recv()
    a = both_cores(ax[...], ar[...])
    ga = g0 * a
    sums2[...] = jnp.zeros_like(sums2)
    sums2[0:1, :] = jnp.sum(a * a, axis=0, keepdims=True)
    sums2[1:2, :] = jnp.sum(r * r, axis=0, keepdims=True)
    sums2[2:3, :] = jnp.sum(r * ga, axis=0, keepdims=True)
    sums2[3:4, :] = jnp.sum(ga * ga, axis=0, keepdims=True)
    c_s2 = [Copy(sums2, sr1.at[k - 1], xp(k)) for k in range(1, 4)]
    for cp in c_s2:
        cp.start()
    next(student)
    for cp in c_s2:
        cp.wait_recv()
    sums3[...] = sums2[...] + sr1[0] + sr1[1] + sr1[2]
    c_s3 = [Copy(sums3, sr2.at[k - 1], zp(k)) for k in range(1, 8)]
    for cp in c_s3:
        cp.start()
    next(student)
    for cp in c_s3:
        cp.wait_recv()
    total = sums3[...] + jnp.sum(sr2[...], axis=0)
    post = lax.rsqrt(total[0:1, :] / DT + 1e-06)
    square = total[1:2, :] + 2.0 * post * total[2:3, :] + post * post * total[3:4, :]
    fin = lax.rsqrt(jnp.maximum(square, 0.0) / DT + 1e-06)
    final = g1 * ((r + ga * post) * fin)
    both = final.astype(bf16)
    mine = pl.ds(pl.multiple_of(y * 128, 128), 128)
    c_y0 = []
    c_y1 = []
    for k in range(1, NY):
        theirs = pl.ds(pl.multiple_of((y - k + NY) % NY * 128, 128), 128)
        for core, out in ((0, c_y0), (1, c_y1)):
            rows = teacher_sel(core, None)[0]
            out.append(Copy(tf.at[z, x, rows, mine], tf.at[z, x, rows, mine], yp(k), tf.at[z, x, rows, theirs]))

    def spread0():
        tf[z, x, 0:TA, mine] = both[0:TA]
        for cp in c_y0:
            cp.start()

    def spread1():
        tf[z, x, TA : 2 * F, mine] = both[TA : 2 * F]
        for cp in c_y1:
            cp.start()

    on_core(0, spread0)
    on_core(1, spread1)
    next(student)

    def spread_wait0():
        for cp in c_y0:
            cp.wait_recv()

    def spread_wait1():
        for cp in c_y1:
            cp.wait_recv()

    on_core(0, spread_wait0)
    on_core(1, spread_wait1)
    next(teacher)
    next(student)
    next(teacher)
    next(student)
    next(teacher)
    next(student)
    next(student)

    local[6].wait()
    for k in range(7):
        cols = slice(k * 512, (k + 1) * 512)
        part = dot(se[:, cols], sf[:, :, :, cols].reshape(TOK, 512), 1, 1)
        sb[...] = part if k == 0 else sb[...] + part
        if k in (0, 1, 2, 4, 6):
            next(teacher)

    local[7].wait()
    for k in range(4):
        part = dot(te[:, k * 1152 : (k + 1) * 1152], tf[2 * k : 2 * k + 2].reshape(1152, TOK), 1, 0)
        tb[...] = part if k == 0 else tb[...] + part

    local[5].wait()
    token = ids[...] - (w * NY + y) * V
    row = lax.broadcasted_iota(jnp.int32, (24, TOK), 0)

    def fold(v):
        return jnp.sum(v.reshape(3, 8, TOK), axis=0)

    def stats(i, carry):
        rows = pl.ds(pl.multiple_of(i * 24, 8), 24)
        u = jnp.tanh(sb[rows, :] * (1.0 / 30.0))
        s = 30.0 * u
        t = 30.0 * jnp.tanh(tb[rows, :] * (1.0 / 30.0))
        es = jnp.exp(s - 30.0)
        et = jnp.exp(t - 30.0)
        sb[rows, :] = 1.0 - u * u
        esb[rows, :] = es
        etb[rows, :] = et
        hit = jnp.where(row + i * 24 == token, s, 0.0)
        return (
            carry[0] + fold(et),
            carry[1] + fold(es),
            carry[2] + fold(et * (t - s)),
            carry[3] + fold(hit),
        )

    zero = jnp.zeros((8, TOK), f32)
    accs = lax.fori_loop(0, V // 24, stats, (zero, zero, zero, zero))
    for i in range(4):
        total_i = jnp.sum(accs[i], axis=0, keepdims=True)
        st[i : i + 1, :] = total_i[:, 0:256]
        st[4 + i : 5 + i, :] = total_i[:, 256:512]
    c_q1 = Copy(st, q1, sib)
    c_q1.start()
    c_q1.wait_recv()
    st2[...] = st[...] + q1[...]
    c_q2 = [Copy(st2, q2.at[k - 1], xyp(k)) for k in range(1, 16)]
    for cp in c_q2:
        cp.start()
    student_drain()
    for cp in [c_sh, c_r, c_a, c_q1] + c_pr + c_s2 + c_s3:
        cp.wait_send()
    for cp in c_q2:
        cp.wait_recv()
    st3[...] = st2[...] + jnp.sum(q2[...], axis=0)
    c_q3 = [Copy(st3, q3.at[k - 1], zp(k)) for k in range(1, 8)]
    for cp in c_q3:
        cp.start()
    teacher_drain()

    def spread_sent0():
        for cp in c_y0:
            cp.wait_send()

    def spread_sent1():
        for cp in c_y1:
            cp.wait_send()

    on_core(0, spread_sent0)
    on_core(1, spread_sent1)
    for cp in c_q2:
        cp.wait_send()
    for cp in c_q3:
        cp.wait_recv()
    packed = st3[...] + jnp.sum(q3[...], axis=0)
    all_stats = jnp.concatenate([packed[0:4], packed[4:8]], axis=1)
    zt, zs = all_stats[0:1, :], all_stats[1:2, :]
    cross, target = all_stats[2:3, :], all_stats[3:4, :]
    log_zs = jnp.log(zs)
    per_token = cross / zt - jnp.log(zt) + log_zs + log_zs + 30.0 - target
    loss_o[0, 0] = jnp.sum(per_token) / TOK

    scale[0:1, :] = 1.0 / zt
    scale[1:2, :] = 2.0 / zs
    for k in range(4):
        cols = slice(k * 128, (k + 1) * 128)
        row_all = lax.broadcasted_iota(jnp.int32, (V, 128), 0)
        onehot = (row_all == token[:, cols]).astype(f32)
        g = scale[1:2, cols] * esb[:, cols] - scale[0:1, cols] * etb[:, cols] - onehot
        g = g * sb[:, cols] * (1.0 / TOK)
        dz[:, cols] = g.astype(bf16)
        dzt[cols, :] = g.T.astype(bf16)

    def product(lo, n, out):
        def step(j, _):
            cols = pl.ds(pl.multiple_of(lo + j * 256, 256), 256)
            val = dot(dzt[...], se[:, cols], 1, 0)
            out(pl.ds(pl.multiple_of(j * 256, 256), 256), val.reshape(NZ, NX, 16, 256))
            return 0

        lax.fori_loop(0, n // 256, step, 0)

    def out_send(cols, val):
        hs[:, :, :, cols] = val.astype(bf16)

    every = slice(None)
    chunks0 = [pl.ds(j, min(512, HA - j)) for j in range(0, HA, 512)]
    c_d0 = [Copy(hs.at[every, every, every, pl.ds(0, HB)], hr.at[every, every, every, pl.ds(0, HB)], sib)]
    c_d1 = [Copy(hs.at[every, every, every, ch], hr.at[every, every, every, ch], sib) for ch in chunks0]
    c_x1 = [
        [Copy(hc.at[every, (x + k) % NX, every, ch], x1r.at[k - 1, every, every, ch], xp(k)) for k in range(1, 4)]
        for ch in chunks0
    ]
    own_b = pl.ds(0, HB)
    c_z1 = [Copy(hc.at[(z + k) % NZ, every, every, own_b], z1r.at[k - 1], zp(k)) for k in (4, 1, 7, 2, 6, 3, 5)]

    def combined(lo, n, at):
        def step(i, _):
            cols = pl.ds(pl.multiple_of(lo + i * 256, 256), 256)
            here = pl.ds(pl.multiple_of(at + i * 256, 256), 256)
            val = dot(dzt[...], se[:, cols], 1, 0).reshape(NZ, NX, 16, 256)
            hc[:, :, :, here] = (val + hr[:, :, :, here].astype(f32)).astype(bf16)
            return 0

        lax.fori_loop(0, n // 256, step, 0)

    def grad0():
        product(HA, HB, out_send)
        c_d0[0].start()
        for j, ch in enumerate(chunks0):
            c_d1[j].wait_recv()
            combined(ch.start, ch.size, ch.start)
            for cp in c_x1[j]:
                cp.start()

    def grad1():
        def part(j):
            ch = chunks0[j]

            def one(cols, val):
                hs[:, :, :, pl.ds(pl.multiple_of(cols.start + ch.start, 256), 256)] = val.astype(bf16)

            product(ch.start, ch.size, one)
            c_d1[j].start()

        part(0)
        part(1)
        c_d0[0].wait_recv()
        combined(HA, HB, 0)
        for cp in c_z1:
            cp.start()
        for j in range(2, len(chunks0)):
            part(j)

    on_core(0, grad0)
    on_core(1, grad1)

    c_eg = []

    def embed(k):
        cols = slice(k * 512, (k + 1) * 512)
        eg[:, cols] = dot(dz[...], sf[:, :, :, cols].reshape(TOK, 512), 1, 0).astype(bf16)
        c_eg.append(pltpu.make_async_copy(eg.at[:, pl.ds(k * 512, 512)], eg_o.at[:, pl.ds(k * 512, 512)], lsem.at[8 + k]))
        c_eg[k].start()

    c_z2 = [[Copy(y1b.at[(z + k) % NZ, every, ch], z2r.at[k - 1, every, ch], zp(k)) for k in range(1, 8)] for ch in chunks0]
    to = [(0, k) for k in range(4)] + [(1, k) for k in range(4)]

    def last(fs, frx, core):
        out = []
        for core_, k in to:
            if core_ == core and k == 0:
                continue
            yy = (y + k) % NY
            out.append(Copy(fs.at[pl.ds(8 * core_ + 2 * yy, 2)], frx.at[k], dev(z, x, core_, yy)))
        return out

    c_f0 = last(fs0, fr0, 0)
    c_f1 = last(fs1, fr1, 1)

    c_x2b = [Copy(y1b.at[(x + k) % NX, every, own_b], x2r.at[k - 1], xp(k)) for k in range(1, 4)]

    def first0(j):
        def fn():
            for cp in c_x1[j]:
                cp.wait_recv()
            cols = chunks0[j]
            val = hc[:, x, :, cols].astype(f32)
            for k in range(3):
                val = val + x1r[k, :, :, cols].astype(f32)
            y1[:, :, cols] = val
            y1b[:, :, cols] = val.astype(bf16)
            for cp in c_z2[j]:
                cp.start()

        return fn

    def turn1():
        for cp in c_z1:
            cp.wait_recv()
        val = hc[z, :, :, own_b].astype(f32)
        for k in range(7):
            val = val + z1r[k].astype(f32)
        y1[0:NX, :, own_b] = val
        y1b[0:NX, :, own_b] = val.astype(bf16)
        for cp in c_x2b:
            cp.start()

    def last1():
        for cp in c_x2b:
            cp.wait_recv()
        val = y1[x, :, 0:HB]
        for k in range(3):
            val = val + x2r[k].astype(f32)
        for t in range(HB // 128):
            fs1[:, t, :] = val[:, t * 128 : (t + 1) * 128]
        for cp in c_f1:
            cp.start()
        fr1[0] = fs1[pl.ds(8 + 2 * y, 2)]

    def last0():
        for j in range(len(chunks0)):
            for cp in c_z2[j]:
                cp.wait_recv()
            cols = chunks0[j]
            val = y1[z, :, cols]
            for k in range(7):
                val = val + z2r[k, :, cols].astype(f32)
            for t in range(cols.size // 128):
                fs0[:, 4 * j + t, :] = val[:, t * 128 : (t + 1) * 128]
        for cp in c_f0:
            cp.start()
        fr0[0] = fs0[pl.ds(2 * y, 2)]

    for k in range(2):
        embed(k)
    for n, (f0, f1) in enumerate(
        [(first0(0), None), (first0(1), None), (first0(2), None), (first0(3), turn1), (first0(4), None)]
    ):
        on_core(0, f0)
        if f1 is not None:
            on_core(1, f1)
        embed(2 + n)
    on_core(0, last0)
    on_core(1, last1)

    for cp in c_q3:
        cp.wait_send()

    def end0():
        for cp in c_d0 + [b for a_ in c_x1 + c_z2 for b in a_]:
            cp.wait_send()

    def end1():
        for cp in c_d1 + c_z1 + c_x2b:
            cp.wait_send()

    on_core(0, end0)
    on_core(1, end1)
    for cp in c_eg:
        cp.wait()

    def arrive(frx, k, i):
        pltpu.make_async_remote_copy(
            src_ref=frx.at[k], dst_ref=frx.at[k], send_sem=ss.at[i], recv_sem=rs.at[i], device_id=sib, device_id_type=MESH
        ).wait_recv()

    def index_of(copies, core, core_, k):
        order = [(a, b) for a, b in to if not (a == core and b == 0)]
        return copies[order.index((core_, k))].i

    def arrive_on(core):
        def fn():
            for k in range(4):
                if not (core == 0 and k == 0):
                    arrive(fr0, k, index_of(c_f0, 0, core, k))
                if not (core == 1 and k == 0):
                    arrive(fr1, k, index_of(c_f1, 1, core, k))

        return fn

    on_core(0, arrive_on(0))
    on_core(1, arrive_on(1))
    head = jnp.sum(fr0[...], axis=0)
    tail = jnp.sum(fr1[...], axis=0)
    for t in range(DS // 128):
        piece = head[:, t, :] if t < HA // 128 else tail[:, t - HA // 128, :]
        hg_o[:, t * 128 : (t + 1) * 128] = piece

    def sent0():
        for cp in c_f0:
            cp.wait_send()

    def sent1():
        for cp in c_f1:
            cp.wait_send()

    on_core(0, sent0)
    on_core(1, sent1)
    assert counter[0] <= NSEM


def body(teacher_attn, out_proj, teacher_resid, norm_gains, teacher_embed, student_hidden, student_embed, token_ids):
    hbm = pl.BlockSpec(memory_space=pl.ANY)
    vm = pl.BlockSpec(memory_space=pltpu.VMEM)
    v = pltpu.VMEM
    loss, hg, eg = pl.pallas_call(
        kernel,
        out_shape=(
            jax.ShapeDtypeStruct((1, 1), f32),
            jax.ShapeDtypeStruct((2, DS), f32),
            jax.ShapeDtypeStruct((V, DS), bf16),
        ),
        in_specs=[hbm] * 8,
        out_specs=(pl.BlockSpec(memory_space=pltpu.SMEM), vm, hbm),
        scratch_shapes=[
            v((TOK, 512), bf16), v((F, 512), bf16), v((F, TOK), bf16), v((2, DT), f32),
            v((V, DT), bf16), v((8, DS), bf16), v((V, DS), bf16), v((1, TOK), jnp.int32),
            v((NZ, NX, 16, DS), bf16), v((NZ, NX, 2 * F, TOK), bf16),
            v((8, DS), f32), v((8, DS), f32),
            v((NY, F, 128), f32), v((NY - 1, F, 128), f32), v((8, TOK), f32),
            v((8, 128), f32), v((8, 128), f32), v((3, 8, 128), f32), v((7, 8, 128), f32),
            v((F, 128), f32), v((F, 128), f32), v((F, 128), f32), v((F, 128), f32),
            v((V, TOK), f32), v((V, TOK), f32), v((V, TOK), f32), v((V, TOK), f32),
            v((8, 256), f32), v((8, 256), f32), v((8, 256), f32),
            v((8, 256), f32), v((15, 8, 256), f32), v((7, 8, 256), f32),
            v((V, TOK), bf16), v((TOK, V), bf16),
            v((NZ, NX, 16, HA), bf16), v((NZ, NX, 16, HA), bf16), v((NZ, NX, 16, HA), bf16),
            v((3, NZ, 16, HA), bf16),
            v((7, NX, 16, HB), bf16),
            v((NZ, 16, HA), f32), v((NZ, 16, HA), bf16), v((7, 16, HA), bf16), v((4, 16, HB), bf16),
            v((16, HA // 128, 128), f32), v((16, HB // 128, 128), f32),
            v((4, 2, HA // 128, 128), f32), v((4, 2, HB // 128, 128), f32),
            v((V, DS), bf16),
            pltpu.SemaphoreType.DMA((15,)),
            pltpu.SemaphoreType.DMA((NSEM,)),
            pltpu.SemaphoreType.DMA((NSEM,)),
        ],
        compiler_params=pltpu.CompilerParams(
            collective_id=0, has_side_effects=True, vmem_limit_bytes=60 * 2**20
        ),
        name="step",
    )(
        teacher_attn, out_proj.T, teacher_resid.T, norm_gains, teacher_embed, student_hidden, student_embed,
        token_ids.reshape(1, TOK),
    )
    return loss.reshape(()), hg, eg


def solution(mesh):
    in_specs = (
        P(None, "narrow"),
        P("narrow", "wide"),
        P(None, "wide"),
        P(),
        P(("wide", "narrow"), None),
        P("wide", None),
        P(("wide", "narrow"), None),
        P(),
    )
    out_specs = (P(), P(("wide", "narrow"), None), P(("wide", "narrow"), None))
    return jax.shard_map(body, mesh=mesh, in_specs=in_specs, out_specs=out_specs, check_vma=False)
```

```python
import jax
import jax.numpy as jnp
from jax import lax
from jax.experimental import pallas as pl
from jax.experimental.pallas import tpu as pltpu
from jax.sharding import PartitionSpec as P

TOK, DT, DS, V, F = 512, 4608, 3584, 504, 72
NZ, NX, NY = 8, 4, 4
SA = 2048
TA = 64
HA = 2816
HB = DS - HA
NSEM = 320
MESH = pl.DeviceIdType.MESH
f32, bf16 = jnp.float32, jnp.bfloat16


def dot(a, b, ca, cb):
    return lax.dot_general(a, b, (((ca,), (cb,)), ((), ())), preferred_element_type=f32)


def kernel(
    attn_h, oproj_h, resid_h, gains_h, te_h, sh_h, se_h, ids_h,
    loss_o, hg_o, eg_o,
    attn, oproj, resid, gains, te, sh, se, ids,
    sf, tf, shx, shr, pt, pr, scale, sums2, sums3, sr1, sr2, rx, rr, ax, ar,
    sb, tb, esb, etb, st, st2, st3, q1, q2, q3, dz, dzt,
    hs, hr, hc, x1r, z1r, y1, y1b, z2r, x2r, fs0, fs1, fr0, fr1, eg,
    lsem, ss, rs,
):
    w = lax.axis_index("wide")
    y = lax.axis_index("narrow")
    z, x, c = w // 8, (w // 2) % 4, w % 2

    def dev(z_, x_, c_, y_):
        return ((z_ * 4 + x_) * 2 + c_, y_)

    def zp(k):
        return dev((z + k + NZ) % NZ, x, c, y)

    def xp(k):
        return dev(z, (x + k + NX) % NX, c, y)

    def yp(k):
        return dev(z, x, c, (y + k) % NY)

    def xyp(k):
        return dev(z, (x + k // 4) % NX, c, (y + k) % NY)

    sib = dev(z, x, 1 - c, y)

    counter = [0]

    def sem():
        counter[0] += 1
        return counter[0] - 1

    class Copy:
        def __init__(self, src, dst, to, landing=None):
            self.src, self.dst, self.to, self.i = src, dst, to, sem()
            self.landing = dst if landing is None else landing

        def make(self, dst):
            return pltpu.make_async_remote_copy(
                src_ref=self.src, dst_ref=dst, send_sem=ss.at[self.i], recv_sem=rs.at[self.i],
                device_id=self.to, device_id_type=MESH,
            )

        def start(self):
            self.make(self.dst).start()

        def wait_send(self):
            self.make(self.dst).wait_send()

        def wait_recv(self):
            self.make(self.landing).wait_recv()

    def on_core(which, fn):
        pl.when(c == which)(fn)

    local = [
        pltpu.make_async_copy(a, b, lsem.at[i])
        for i, (a, b) in enumerate(
            [(sh_h, sh), (attn_h, attn), (oproj_h, oproj), (resid_h, resid), (gains_h, gains), (ids_h, ids), (se_h, se), (te_h, te)]
        )
    ]
    for cp in local:
        cp.start()

    barrier = pltpu.get_barrier_semaphore()
    peers = [zp(k) for k in range(1, 8)] + [xyp(k) for k in range(1, 16)] + [sib]
    peers += [dev(z, x, 1 - c, (y + k) % NY) for k in range(1, 4)]
    for p in peers:
        pl.semaphore_signal(barrier, inc=1, device_id=p, device_id_type=MESH)
    local[0].wait()
    shx[...] = sh[...].astype(f32)
    c_sh = Copy(shx, shr, sib)
    local[3].wait()
    rx[...] = resid[:, pl.ds(pl.multiple_of(y * 128, 128), 128)].astype(f32)
    c_r = Copy(rx, rr, sib)

    def ring(n, pos, peer, block, half):
        m = n // 2
        waits, starts, every = {}, {}, []
        for s in range(1, m + 1):
            last = s == m
            pick = half if last else (lambda i, h: block(i))
            r = Copy(pick((pos - s + 1 + n) % n, 0), pick((pos - s + 1 + n) % n, 0), peer(1), pick((pos - s + n) % n, 0))
            l = Copy(pick((pos + s - 1) % n, 1), pick((pos + s - 1) % n, 1), peer(-1), pick((pos + s) % n, 1))
            starts[s] = [r.start, l.start]
            waits[s] = [r.wait_recv, l.wait_recv]
            every += [r.wait_send, l.wait_send]
        return starts, waits, every

    near = (1, -1, 2, -2, 3, -3, 4)

    def gather(buf, sel):
        def at(i, j, core, h=None):
            rows, cols = sel(core, h)
            return buf.at[i, j, rows, cols]

        every = slice(None)

        def zi(k):
            return (z + k + NZ) % NZ

        def xi(k):
            return (x + k + NX) % NX

        z0 = ring(NZ, z, zp, lambda i: at(i, x, 0), lambda i, h: at(i, x, 0, h))
        x0 = {
            (d, k): Copy(at(zi(d), x, 0), at(zi(d), x, 0), xp(k), at(zi(d), xi(-k), 0))
            for d in (0,) + near for k in (1, 2, 3)
        }
        s0 = {k: Copy(at(every, xi(-k), 0), at(every, xi(-k), 0), sib) for k in (0, 1, 3, 2)}

        def fan(*ds):
            return [x0[d, k].start for d in ds for k in (1, 3, 2)]

        def landed(k):
            return [x0[d, k].wait_recv for d in (0,) + near]

        steps0 = [
            z0[0][1] + fan(0),
            z0[1][1] + z0[0][2] + fan(1, -1),
            z0[1][2] + z0[0][3] + fan(2, -2),
            z0[1][3] + z0[0][4] + fan(3, -3),
            z0[1][4] + fan(4) + [s0[0].start],
            landed(1) + [s0[1].start] + landed(3) + [s0[3].start],
            landed(2) + [s0[2].start],
        ]
        x1 = {k: Copy(at(z, x, 1), at(z, x, 1), xp(k), at(z, xi(-k), 1)) for k in (1, 3, 2)}
        z1 = {
            k: ring(NZ, z, zp, lambda i, k=k: at(i, xi(-k), 1), lambda i, h, k=k: at(i, xi(-k), 1, h)) for k in (0, 1, 3, 2)
        }
        s1 = {k: Copy(at(zi(k), every, 1), at(zi(k), every, 1), sib) for k in (0,) + near}

        def onward(n):
            out = []
            for k in (0, 1, 3, 2):
                out += z1[k][1][n]
                if n < 4:
                    out += z1[k][0][n + 1]
            return out

        steps1 = [
            [x1[k].start for k in x1] + z1[0][0][1],
            sum([[x1[k].wait_recv] + z1[k][0][1] for k in x1], []) + [s1[0].start],
            onward(1) + [s1[1].start, s1[-1].start],
            onward(2) + [s1[2].start, s1[-2].start],
            onward(3) + [s1[3].start, s1[-3].start],
            onward(4) + [s1[4].start],
            [],
        ]
        steps0.append([s1[k].wait_recv for k in s1])
        steps1.append([s0[k].wait_recv for k in s0])
        drain0 = z0[2] + [x0[i].wait_send for i in x0] + [s0[k].wait_send for k in s0]
        drain1 = [x1[k].wait_send for k in x1] + sum([z1[k][2] for k in z1], []) + [s1[k].wait_send for k in s1]

        def emit(fns0, fns1):
            def run0():
                for fn in fns0:
                    fn()

            def run1():
                for fn in fns1:
                    fn()

            on_core(0, run0)
            on_core(1, run1)

        def gen():
            for a, b in zip(steps0, steps1):
                emit(a, b)
                yield

        return gen(), lambda: emit(drain0, drain1)

    def student_sel(core, h):
        lo, hi = (0, SA) if core == 0 else (SA, DS)
        if h is not None:
            mid = (lo + hi) // 2
            lo, hi = (lo, mid) if h == 0 else (mid, hi)
        return slice(None), pl.ds(lo, hi - lo)

    def teacher_sel(core, h):
        rows = pl.ds(0, TA) if core == 0 else pl.ds(TA, 2 * F - TA)
        return rows, slice(None) if h is None else pl.ds(h * 256, 256)

    student, student_drain = gather(sf, student_sel)
    teacher, teacher_drain = gather(tf, teacher_sel)

    local[1].wait()
    local[2].wait()
    proj = dot(oproj[...], attn[...], 1, 1)
    for b in range(NY):
        pt[b] = proj[:, b * 128 : (b + 1) * 128]
    c_pr = [Copy(pt.at[(y + k) % NY], pr.at[k - 1], yp(k)) for k in range(1, NY)]
    local[4].wait()
    feature = (w // 2) * 2 * F + lax.broadcasted_iota(jnp.int32, (2 * F, 128), 0)
    lane = lax.broadcasted_iota(jnp.int32, (2 * F, 128), 1)

    def pick_gains(i, carry):
        part = gains[:, pl.ds(pl.multiple_of(i * 128, 128), 128)]
        here = (lane + i * 128) == feature
        return carry[0] + jnp.where(here, part[0:1, :], 0.0), carry[1] + jnp.where(here, part[1:2, :], 0.0)

    none = jnp.zeros((2 * F, 128), f32)
    g0, g1 = lax.fori_loop(0, DT // 128, pick_gains, (none, none))
    g0 = jnp.sum(g0, axis=1, keepdims=True)
    g1 = jnp.sum(g1, axis=1, keepdims=True)

    pl.semaphore_wait(barrier, len(peers))
    c_sh.start()
    for cp in c_pr:
        cp.start()
    c_r.start()

    c_sh.wait_recv()
    first = jnp.where(c == 0, shx[...], shr[...])
    second = jnp.where(c == 0, shr[...], shx[...])
    block = jnp.concatenate([first, second], axis=0).astype(bf16)

    def put0():
        sf[z, x, :, 0:SA] = block[:, 0:SA]

    def put1():
        sf[z, x, :, SA:DS] = block[:, SA:DS]

    on_core(0, put0)
    on_core(1, put1)
    next(student)

    def both_cores(own, other):
        return jnp.concatenate([jnp.where(c == 0, own, other), jnp.where(c == 0, other, own)], axis=0)

    for cp in c_pr:
        cp.wait_recv()
    a = pt[y] + pr[0] + pr[1] + pr[2]
    ax[...] = a.astype(bf16).astype(f32)
    c_a = Copy(ax, ar, sib)
    c_a.start()
    c_r.wait_recv()
    r = both_cores(rx[...], rr[...])
    c_a.wait_recv()
    a = both_cores(ax[...], ar[...])
    ga = g0 * a
    sums2[...] = jnp.zeros_like(sums2)
    sums2[0:1, :] = jnp.sum(a * a, axis=0, keepdims=True)
    sums2[1:2, :] = jnp.sum(r * r, axis=0, keepdims=True)
    sums2[2:3, :] = jnp.sum(r * ga, axis=0, keepdims=True)
    sums2[3:4, :] = jnp.sum(ga * ga, axis=0, keepdims=True)
    c_s2 = [Copy(sums2, sr1.at[k - 1], xp(k)) for k in range(1, 4)]
    for cp in c_s2:
        cp.start()
    next(student)
    for cp in c_s2:
        cp.wait_recv()
    sums3[...] = sums2[...] + sr1[0] + sr1[1] + sr1[2]
    c_s3 = [Copy(sums3, sr2.at[k - 1], zp(k)) for k in range(1, 8)]
    for cp in c_s3:
        cp.start()
    next(student)
    for cp in c_s3:
        cp.wait_recv()
    total = sums3[...] + jnp.sum(sr2[...], axis=0)
    post = lax.rsqrt(total[0:1, :] / DT + 1e-06)
    square = total[1:2, :] + 2.0 * post * total[2:3, :] + post * post * total[3:4, :]
    fin = lax.rsqrt(jnp.maximum(square, 0.0) / DT + 1e-06)
    final = g1 * ((r + ga * post) * fin)
    both = final.astype(bf16)
    mine = pl.ds(pl.multiple_of(y * 128, 128), 128)
    c_y0 = []
    c_y1 = []
    for k in range(1, NY):
        theirs = pl.ds(pl.multiple_of((y - k + NY) % NY * 128, 128), 128)
        for core, out in ((0, c_y0), (1, c_y1)):
            rows = teacher_sel(core, None)[0]
            out.append(Copy(tf.at[z, x, rows, mine], tf.at[z, x, rows, mine], yp(k), tf.at[z, x, rows, theirs]))

    def spread0():
        tf[z, x, 0:TA, mine] = both[0:TA]
        for cp in c_y0:
            cp.start()

    def spread1():
        tf[z, x, TA : 2 * F, mine] = both[TA : 2 * F]
        for cp in c_y1:
            cp.start()

    on_core(0, spread0)
    on_core(1, spread1)
    next(student)

    def spread_wait0():
        for cp in c_y0:
            cp.wait_recv()

    def spread_wait1():
        for cp in c_y1:
            cp.wait_recv()

    on_core(0, spread_wait0)
    on_core(1, spread_wait1)
    next(teacher)
    next(student)
    next(teacher)
    next(student)
    next(teacher)
    next(student)
    next(student)

    local[6].wait()
    for k in range(7):
        cols = slice(k * 512, (k + 1) * 512)
        part = dot(se[:, cols], sf[:, :, :, cols].reshape(TOK, 512), 1, 1)
        sb[...] = part if k == 0 else sb[...] + part
        if k in (0, 1, 2, 4, 6):
            next(teacher)

    local[7].wait()
    for k in range(4):
        part = dot(te[:, k * 1152 : (k + 1) * 1152], tf[2 * k : 2 * k + 2].reshape(1152, TOK), 1, 0)
        tb[...] = part if k == 0 else tb[...] + part

    local[5].wait()
    token = ids[...] - (w * NY + y) * V
    row = lax.broadcasted_iota(jnp.int32, (24, TOK), 0)

    def fold(v):
        return jnp.sum(v.reshape(3, 8, TOK), axis=0)

    def stats(i, carry):
        rows = pl.ds(pl.multiple_of(i * 24, 8), 24)
        u = jnp.tanh(sb[rows, :] * (1.0 / 30.0))
        s = 30.0 * u
        t = 30.0 * jnp.tanh(tb[rows, :] * (1.0 / 30.0))
        es = jnp.exp(s - 30.0)
        et = jnp.exp(t - 30.0)
        sb[rows, :] = 1.0 - u * u
        esb[rows, :] = es
        etb[rows, :] = et
        hit = jnp.where(row + i * 24 == token, s, 0.0)
        return (
            carry[0] + fold(et),
            carry[1] + fold(es),
            carry[2] + fold(et * (t - s)),
            carry[3] + fold(hit),
        )

    zero = jnp.zeros((8, TOK), f32)
    accs = lax.fori_loop(0, V // 24, stats, (zero, zero, zero, zero))
    for i in range(4):
        total_i = jnp.sum(accs[i], axis=0, keepdims=True)
        st[i : i + 1, :] = total_i[:, 0:256]
        st[4 + i : 5 + i, :] = total_i[:, 256:512]
    c_q1 = Copy(st, q1, sib)
    c_q1.start()
    c_q1.wait_recv()
    st2[...] = st[...] + q1[...]
    c_q2 = [Copy(st2, q2.at[k - 1], xyp(k)) for k in range(1, 16)]
    for cp in c_q2:
        cp.start()
    student_drain()
    for cp in [c_sh, c_r, c_a, c_q1] + c_pr + c_s2 + c_s3:
        cp.wait_send()
    for cp in c_q2:
        cp.wait_recv()
    st3[...] = st2[...] + jnp.sum(q2[...], axis=0)
    c_q3 = [Copy(st3, q3.at[k - 1], zp(k)) for k in range(1, 8)]
    for cp in c_q3:
        cp.start()
    teacher_drain()

    def spread_sent0():
        for cp in c_y0:
            cp.wait_send()

    def spread_sent1():
        for cp in c_y1:
            cp.wait_send()

    on_core(0, spread_sent0)
    on_core(1, spread_sent1)
    for cp in c_q2:
        cp.wait_send()
    for cp in c_q3:
        cp.wait_recv()
    packed = st3[...] + jnp.sum(q3[...], axis=0)
    all_stats = jnp.concatenate([packed[0:4], packed[4:8]], axis=1)
    zt, zs = all_stats[0:1, :], all_stats[1:2, :]
    cross, target = all_stats[2:3, :], all_stats[3:4, :]
    log_zs = jnp.log(zs)
    per_token = cross / zt - jnp.log(zt) + log_zs + log_zs + 30.0 - target
    loss_o[0, 0] = jnp.sum(per_token) / TOK

    scale[0:1, :] = 1.0 / zt
    scale[1:2, :] = 2.0 / zs
    for k in range(4):
        cols = slice(k * 128, (k + 1) * 128)
        row_all = lax.broadcasted_iota(jnp.int32, (V, 128), 0)
        onehot = (row_all == token[:, cols]).astype(f32)
        g = scale[1:2, cols] * esb[:, cols] - scale[0:1, cols] * etb[:, cols] - onehot
        g = g * sb[:, cols] * (1.0 / TOK)
        dz[:, cols] = g.astype(bf16)
        dzt[cols, :] = g.T.astype(bf16)

    def product(lo, n, out):
        def step(j, _):
            cols = pl.ds(pl.multiple_of(lo + j * 256, 256), 256)
            val = dot(dzt[...], se[:, cols], 1, 0)
            out(pl.ds(pl.multiple_of(j * 256, 256), 256), val.reshape(NZ, NX, 16, 256))
            return 0

        lax.fori_loop(0, n // 256, step, 0)

    def out_send(cols, val):
        hs[:, :, :, cols] = val.astype(bf16)

    every = slice(None)
    chunks0 = [pl.ds(j, min(512, HA - j)) for j in range(0, HA, 512)]
    c_d0 = [Copy(hs.at[every, every, every, pl.ds(0, HB)], hr.at[every, every, every, pl.ds(0, HB)], sib)]
    c_d1 = [Copy(hs.at[every, every, every, ch], hr.at[every, every, every, ch], sib) for ch in chunks0]
    c_x1 = [
        [Copy(hc.at[every, (x + k) % NX, every, ch], x1r.at[k - 1, every, every, ch], xp(k)) for k in range(1, 4)]
        for ch in chunks0
    ]
    own_b = pl.ds(0, HB)
    c_z1 = [Copy(hc.at[(z + k) % NZ, every, every, own_b], z1r.at[k - 1], zp(k)) for k in (4, 1, 7, 2, 6, 3, 5)]

    def combined(lo, n, at):
        def step(i, _):
            cols = pl.ds(pl.multiple_of(lo + i * 256, 256), 256)
            here = pl.ds(pl.multiple_of(at + i * 256, 256), 256)
            val = dot(dzt[...], se[:, cols], 1, 0).reshape(NZ, NX, 16, 256)
            hc[:, :, :, here] = (val + hr[:, :, :, here].astype(f32)).astype(bf16)
            return 0

        lax.fori_loop(0, n // 256, step, 0)

    def grad0():
        product(HA, HB, out_send)
        c_d0[0].start()
        for j, ch in enumerate(chunks0):
            c_d1[j].wait_recv()
            combined(ch.start, ch.size, ch.start)
            for cp in c_x1[j]:
                cp.start()

    def grad1():
        def part(j):
            ch = chunks0[j]

            def one(cols, val):
                hs[:, :, :, pl.ds(pl.multiple_of(cols.start + ch.start, 256), 256)] = val.astype(bf16)

            product(ch.start, ch.size, one)
            c_d1[j].start()

        part(0)
        part(1)
        c_d0[0].wait_recv()
        combined(HA, HB, 0)
        for cp in c_z1:
            cp.start()
        for j in range(2, len(chunks0)):
            part(j)

    on_core(0, grad0)
    on_core(1, grad1)

    c_eg = []

    def embed(k):
        cols = slice(k * 512, (k + 1) * 512)
        eg[:, cols] = dot(dz[...], sf[:, :, :, cols].reshape(TOK, 512), 1, 0).astype(bf16)
        c_eg.append(pltpu.make_async_copy(eg.at[:, pl.ds(k * 512, 512)], eg_o.at[:, pl.ds(k * 512, 512)], lsem.at[8 + k]))
        c_eg[k].start()

    c_z2 = [[Copy(y1b.at[(z + k) % NZ, every, ch], z2r.at[k - 1, every, ch], zp(k)) for k in range(1, 8)] for ch in chunks0]
    to = [(0, k) for k in range(4)] + [(1, k) for k in range(4)]

    def last(fs, frx, core):
        out = []
        for core_, k in to:
            if core_ == core and k == 0:
                continue
            yy = (y + k) % NY
            out.append(Copy(fs.at[pl.ds(8 * core_ + 2 * yy, 2)], frx.at[k], dev(z, x, core_, yy)))
        return out

    c_f0 = last(fs0, fr0, 0)
    c_f1 = last(fs1, fr1, 1)

    c_x2b = [Copy(y1b.at[(x + k) % NX, every, own_b], x2r.at[k - 1], xp(k)) for k in range(1, 4)]

    def first0(j):
        def fn():
            for cp in c_x1[j]:
                cp.wait_recv()
            cols = chunks0[j]
            val = hc[:, x, :, cols].astype(f32)
            for k in range(3):
                val = val + x1r[k, :, :, cols].astype(f32)
            y1[:, :, cols] = val
            y1b[:, :, cols] = val.astype(bf16)
            for cp in c_z2[j]:
                cp.start()

        return fn

    def turn1():
        for cp in c_z1:
            cp.wait_recv()
        val = hc[z, :, :, own_b].astype(f32)
        for k in range(7):
            val = val + z1r[k].astype(f32)
        y1[0:NX, :, own_b] = val
        y1b[0:NX, :, own_b] = val.astype(bf16)
        for cp in c_x2b:
            cp.start()

    def last1():
        for cp in c_x2b:
            cp.wait_recv()
        val = y1[x, :, 0:HB]
        for k in range(3):
            val = val + x2r[k].astype(f32)
        for t in range(HB // 128):
            fs1[:, t, :] = val[:, t * 128 : (t + 1) * 128]
        for cp in c_f1:
            cp.start()
        fr1[0] = fs1[pl.ds(8 + 2 * y, 2)]

    def last0():
        for j in range(len(chunks0)):
            for cp in c_z2[j]:
                cp.wait_recv()
            cols = chunks0[j]
            val = y1[z, :, cols]
            for k in range(7):
                val = val + z2r[k, :, cols].astype(f32)
            for t in range(cols.size // 128):
                fs0[:, 4 * j + t, :] = val[:, t * 128 : (t + 1) * 128]
        for cp in c_f0:
            cp.start()
        fr0[0] = fs0[pl.ds(2 * y, 2)]

    for k in range(2):
        embed(k)
    for n, (f0, f1) in enumerate(
        [
            (first0(0), None), (first0(1), None), (first0(2), turn1),
            (first0(3), None), (first0(4), last1), (first0(5), None),
        ]
    ):
        on_core(0, f0)
        if f1 is not None:
            on_core(1, f1)
        if n < 5:
            embed(2 + n)
    on_core(0, last0)

    for cp in c_q3:
        cp.wait_send()

    def end0():
        for cp in c_d0 + [b for a_ in c_x1 + c_z2 for b in a_]:
            cp.wait_send()

    def end1():
        for cp in c_d1 + c_z1 + c_x2b:
            cp.wait_send()

    on_core(0, end0)
    on_core(1, end1)
    for cp in c_eg:
        cp.wait()

    def arrive(frx, k, i):
        pltpu.make_async_remote_copy(
            src_ref=frx.at[k], dst_ref=frx.at[k], send_sem=ss.at[i], recv_sem=rs.at[i], device_id=sib, device_id_type=MESH
        ).wait_recv()

    def index_of(copies, core, core_, k):
        order = [(a, b) for a, b in to if not (a == core and b == 0)]
        return copies[order.index((core_, k))].i

    def arrive_on(core):
        def fn():
            for k in range(4):
                if not (core == 0 and k == 0):
                    arrive(fr0, k, index_of(c_f0, 0, core, k))
                if not (core == 1 and k == 0):
                    arrive(fr1, k, index_of(c_f1, 1, core, k))

        return fn

    on_core(0, arrive_on(0))
    on_core(1, arrive_on(1))
    head = jnp.sum(fr0[...], axis=0)
    tail = jnp.sum(fr1[...], axis=0)
    for t in range(DS // 128):
        piece = head[:, t, :] if t < HA // 128 else tail[:, t - HA // 128, :]
        hg_o[:, t * 128 : (t + 1) * 128] = piece

    def sent0():
        for cp in c_f0:
            cp.wait_send()

    def sent1():
        for cp in c_f1:
            cp.wait_send()

    on_core(0, sent0)
    on_core(1, sent1)
    assert counter[0] <= NSEM


def body(teacher_attn, out_proj, teacher_resid, norm_gains, teacher_embed, student_hidden, student_embed, token_ids):
    hbm = pl.BlockSpec(memory_space=pl.ANY)
    vm = pl.BlockSpec(memory_space=pltpu.VMEM)
    v = pltpu.VMEM
    loss, hg, eg = pl.pallas_call(
        kernel,
        out_shape=(
            jax.ShapeDtypeStruct((1, 1), f32),
            jax.ShapeDtypeStruct((2, DS), f32),
            jax.ShapeDtypeStruct((V, DS), bf16),
        ),
        in_specs=[hbm] * 8,
        out_specs=(pl.BlockSpec(memory_space=pltpu.SMEM), vm, hbm),
        scratch_shapes=[
            v((TOK, 512), bf16), v((F, 512), bf16), v((F, TOK), bf16), v((2, DT), f32),
            v((V, DT), bf16), v((8, DS), bf16), v((V, DS), bf16), v((1, TOK), jnp.int32),
            v((NZ, NX, 16, DS), bf16), v((NZ, NX, 2 * F, TOK), bf16),
            v((8, DS), f32), v((8, DS), f32),
            v((NY, F, 128), f32), v((NY - 1, F, 128), f32), v((8, TOK), f32),
            v((8, 128), f32), v((8, 128), f32), v((3, 8, 128), f32), v((7, 8, 128), f32),
            v((F, 128), f32), v((F, 128), f32), v((F, 128), f32), v((F, 128), f32),
            v((V, TOK), f32), v((V, TOK), f32), v((V, TOK), f32), v((V, TOK), f32),
            v((8, 256), f32), v((8, 256), f32), v((8, 256), f32),
            v((8, 256), f32), v((15, 8, 256), f32), v((7, 8, 256), f32),
            v((V, TOK), bf16), v((TOK, V), bf16),
            v((NZ, NX, 16, HA), bf16), v((NZ, NX, 16, HA), bf16), v((NZ, NX, 16, HA), bf16),
            v((3, NZ, 16, HA), bf16),
            v((7, NX, 16, HB), bf16),
            v((NZ, 16, HA), f32), v((NZ, 16, HA), bf16), v((7, 16, HA), bf16), v((4, 16, HB), bf16),
            v((16, HA // 128, 128), f32), v((16, HB // 128, 128), f32),
            v((4, 2, HA // 128, 128), f32), v((4, 2, HB // 128, 128), f32),
            v((V, DS), bf16),
            pltpu.SemaphoreType.DMA((15,)),
            pltpu.SemaphoreType.DMA((NSEM,)),
            pltpu.SemaphoreType.DMA((NSEM,)),
        ],
        compiler_params=pltpu.CompilerParams(
            collective_id=0, has_side_effects=True, vmem_limit_bytes=60 * 2**20
        ),
        name="step",
    )(
        teacher_attn, out_proj.T, teacher_resid.T, norm_gains, teacher_embed, student_hidden, student_embed,
        token_ids.reshape(1, TOK),
    )
    return loss.reshape(()), hg, eg


def solution(mesh):
    in_specs = (
        P(None, "narrow"),
        P("narrow", "wide"),
        P(None, "wide"),
        P(),
        P(("wide", "narrow"), None),
        P("wide", None),
        P(("wide", "narrow"), None),
        P(),
    )
    out_specs = (P(), P(("wide", "narrow"), None), P(("wide", "narrow"), None))
    return jax.shard_map(body, mesh=mesh, in_specs=in_specs, out_specs=out_specs, check_vma=False)
```
